256 devices in a mesh: ch: 4 (over x_hi, core), tile: 64 (over y, z, x_lo).
Axes of the slice: x: 4 (x_hi: 2, x_lo: 2; x = x_hi * 2 + x_lo), y: 4, z: 8, core: 2. Of those that a mesh axis runs over, the one named last changes fastest.
Arguments:
- frames: bfloat16 [2, 64, 32, 56, 512], P(None, 'tile', None, None, 'ch'), may hold values from -6 to 6
- cached: bfloat16 [2, 64, 32, 56, 512], P(None, 'tile', None, None, 'ch'), may hold values from -6 to 6
- weight: bfloat16 [3, 3, 3, 512, 512], P(None, None, None, 'ch'), may hold values from -0.0546875 to 0.0546875
- out_bias: float32 [512], P('ch'), may hold values from -3 to 3
Outputs:
- activated: bfloat16 [2, 64, 32, 56, 512], P(None, 'tile', None, None, 'ch')
The draws below stay inside these ranges and needn't reach their ends.
All inputs are finite; a program needn't handle non-finite values.
Results may differ from the reference program's by a relative error of at most 0.0023.
Values may be sent and summed in bfloat16 or wider, within the bound.
A program may use at most 64 MiB of HBM per device.

```python
import jax
import jax.numpy as jnp
from jax import lax

CIN = 512
COUT = 512
FRAMES = 2
CACHE = 2
GX = 8
TH = 32
TW = 56
TILES = 64


def levels(own_key, extent, pieces, smallest, high):
    level = 1.0
    for position, parts in pieces:
        draws = jax.random.uniform(jax.random.fold_in(jax.random.fold_in(own_key, 6), position), (parts,), jnp.float32, smallest / len(pieces), high / len(pieces))
        level = level * jnp.repeat(jnp.exp(draws), extent[position] // parts).reshape((-1,) + (1,) * (len(extent) - 1 - position))
    return level


def normal_values(own_key, extent, deviation, bound, shards=(), held_as=jnp.bfloat16):
    level = levels(own_key, extent, shards, -0.22, 0.18) if shards else 1.0
    values = jax.random.normal(own_key, extent, jnp.float32) * deviation * level
    return jnp.minimum(jnp.maximum(values, -bound), bound).astype(held_as)


def setup_inputs(seed: int = 0) -> dict:
    splits = jax.random.split(jax.random.key(seed), 5)
    return {
        "frames": normal_values(splits[0], (FRAMES, TILES, TH, TW, CIN), 1.0, 6.0, ((1, 64), (4, 4))),
        "cached": normal_values(splits[1], (CACHE, TILES, TH, TW, CIN), 1.0, 6.0, ((1, 64), (4, 4))),
        "weight": normal_values(splits[2], (3, 3, 3, CIN, COUT), (27 * CIN) ** -0.5, 0.0546875, ((3, 4),)),
        "out_bias": normal_values(splits[3], (COUT,), 0.5, 3.0, ((0, 4),), jnp.float32),
    }


def untile(field):
    frame_count = field.shape[0]
    chan_count = field.shape[-1]
    grid_rows = TILES // GX
    field = field.reshape(frame_count, grid_rows, GX, TH, TW, chan_count)
    field = field.transpose(0, 1, 3, 2, 4, 5)
    return field.reshape(frame_count, grid_rows * TH, GX * TW, chan_count)


def retile(field):
    frame_count = field.shape[0]
    chan_count = field.shape[-1]
    grid_rows = TILES // GX
    field = field.reshape(frame_count, grid_rows, TH, GX, TW, chan_count)
    field = field.transpose(0, 1, 3, 2, 4, 5)
    return field.reshape(frame_count, TILES, TH, TW, chan_count)


def reference(frames, cached, weight, out_bias):
    stacked = jnp.concatenate([untile(cached), untile(frames)], axis=0)
    height = stacked.shape[1]
    breadth = stacked.shape[2]
    padded = jnp.pad(stacked, ((0, 0), (1, 1), (1, 1), (0, 0)))
    summed = jnp.zeros((FRAMES * height * breadth, COUT), jnp.float32)
    for shift_t in range(3):
        for shift_y in range(3):
            for shift_x in range(3):
                window = padded[shift_t:shift_t + FRAMES, shift_y:shift_y + height, shift_x:shift_x + breadth, :]
                window = window.reshape(FRAMES * height * breadth, CIN).astype(jnp.float32)
                taps = weight[shift_t, shift_y, shift_x].astype(jnp.float32)
                summed = summed + jnp.dot(window, taps, precision=lax.Precision.HIGHEST, preferred_element_type=jnp.float32)
    preact = summed + out_bias[None, :]
    activated = jax.nn.silu(preact).astype(jnp.bfloat16)
    return retile(activated.reshape(FRAMES, height, breadth, COUT))
```

```python
import jax
import jax.numpy as jnp
from jax import lax
from jax.experimental import pallas as pl
from jax.experimental.pallas import tpu as pltpu
from jax.sharding import PartitionSpec as P

GX = 8
GY = 8
TH = 32
TW = 56
CB = 128
PIX = TH * TW
RB = 4
NB = TH // RB
BR = RB * TW
MB = 2 * BR
PAIR = 2 * TW
SCALE = 2.0**20
MESH = pl.DeviceIdType.MESH
TAPS = [(a, b, e) for a in range(3) for b in range(3) for e in range(3)]


def encode(v):
    s = v * SCALE
    return ((s * s) * (s * jnp.abs(s))).astype(jnp.bfloat16)


def decode(w):
    w = w.astype(jnp.float32)
    root = jnp.sqrt(jnp.sqrt(jnp.abs(w))) * (1.0 / SCALE)
    return jnp.where(w < 0, -root, root)


def sideways(v, left, right):
    lane = lax.broadcasted_iota(jnp.int32, (8, CB), 0)
    m = pltpu.roll(v, 1, 0)
    p = pltpu.roll(v, TW - 1, 0)
    m = jnp.concatenate([jnp.where(lane == 0, left, m[:8]), m[8:]], axis=0)
    p = jnp.concatenate([p[:-8], jnp.where(lane == 7, right, p[-8:])], axis=0)
    return m, v, p


def kernel(cached, frames, weight, bias, out, xe, xo, wr, wl, edge_l, edge_r, halo_l, halo_r, left_f, right_f, halo_a, halo_b,
           corner_up, corner_dn, corner_a, corner_b, core_out, core_in, keep, cross_out, cross_in, out_v,
           in_sem, halo_ss, halo_rs, core_ss, core_rs, cross_ss, cross_rs, out_sem):
    ch = lax.axis_index("ch")
    tile = lax.axis_index("tile")
    h, c = ch // 2, ch % 2
    row, col = tile // GX, tile % GX
    left = (ch, row * GX + (col + GX - 1) % GX)
    right = (ch, row * GX + (col + 1) % GX)
    up = (ch, ((row + GY - 1) % GY) * GX + col)
    down = (ch, ((row + 1) % GY) * GX + col)
    mate = (h * 2 + (1 - c), tile)
    across = ((1 - h) * 2 + c, tile)

    loads = [
        pltpu.make_async_copy(cached, xo.at[1, pl.ds(0, 2)], in_sem.at[0]),
        pltpu.make_async_copy(frames, xo.at[1, pl.ds(2, 2)], in_sem.at[1]),
    ]
    for i, (dst, half, group) in enumerate([(wr, 0, (1 - h) * 2 + 1 - c), (wr, 1, (1 - h) * 2 + c), (wl, 0, h * 2 + 1 - c), (wl, 1, ch)]):
        loads.append(pltpu.make_async_copy(
            weight.at[:, pl.ds(pl.multiple_of(group * CB, CB), CB)], dst.at[:, pl.ds(half * CB, CB)], in_sem.at[2 + i]))
    for load in loads:
        load.start()

    barrier = pltpu.get_barrier_semaphore()
    for device in (left, right, up, down, mate, across):
        pl.semaphore_signal(barrier, inc=1, device_id=device, device_id_type=MESH)
    loads[0].wait()
    loads[1].wait()

    lane = lax.broadcasted_iota(jnp.int32, (8, CB), 0)

    @pl.loop(0, 4)
    def _(f):
        for g in range(2):
            acc_l = [jnp.zeros((8, CB), jnp.float32)] * 2
            acc_r = [jnp.zeros((8, CB), jnp.float32)] * 2
            for q in range(8):
                at = (g * 8 + q) * PAIR
                first = xo[1, f, at:at + 16, :].astype(jnp.float32)
                middle = xo[1, f, at + 48:at + 64, :].astype(jnp.float32)
                last = xo[1, f, at + 96:at + 112, :].astype(jnp.float32)
                k, d = (2 * q) // 8, (2 * q) % 8
                acc_l[k] = jnp.where(lane == d, first[0:1], acc_l[k])
                acc_r[k] = jnp.where(lane == d, middle[7:8], acc_r[k])
                acc_l[k] = jnp.where(lane == d + 1, middle[8:9], acc_l[k])
                acc_r[k] = jnp.where(lane == d + 1, last[15:16], acc_r[k])
            at = pl.ds(pl.multiple_of(f * TH + g * 16, 16), 16)
            edge_l[at, :] = jnp.concatenate(acc_l, axis=0).astype(jnp.bfloat16)
            edge_r[at, :] = jnp.concatenate(acc_r, axis=0).astype(jnp.bfloat16)

    pl.semaphore_wait(barrier, 6)

    def remote(src, dst, ss, rs, device):
        return pltpu.make_async_remote_copy(src_ref=src, dst_ref=dst, send_sem=ss, recv_sem=rs, device_id=device, device_id_type=MESH)

    to_left = remote(edge_l, halo_r, halo_ss.at[0], halo_rs.at[0], left)
    to_right = remote(edge_r, halo_l, halo_ss.at[1], halo_rs.at[1], right)
    to_up = remote(xo.at[1, :, pl.ds(0, 64)], halo_b, halo_ss.at[2], halo_rs.at[2], up)
    to_down = remote(xo.at[1, :, pl.ds(PIX - 64, 64)], halo_a, halo_ss.at[3], halo_rs.at[3], down)
    to_left.start()
    to_right.start()
    to_up.start()
    to_down.start()
    to_left.wait_recv()
    to_right.wait_recv()
    left_f[...] = jnp.where(col > 0, halo_l[...].astype(jnp.float32), 0.0)
    right_f[...] = jnp.where(col < GX - 1, halo_r[...].astype(jnp.float32), 0.0)

    for ref, r in ((corner_up, 0), (corner_dn, TH - 1)):
        pieces = []
        for f in range(4):
            pieces += [left_f[f * TH + r:f * TH + r + 1, :], right_f[f * TH + r:f * TH + r + 1, :]]
        ref[...] = jnp.concatenate(pieces + [jnp.zeros((8, CB), jnp.float32)], axis=0).astype(jnp.bfloat16)
    corner_to_up = remote(corner_up, corner_b, halo_ss.at[4], halo_rs.at[4], up)
    corner_to_down = remote(corner_dn, corner_a, halo_ss.at[5], halo_rs.at[5], down)
    corner_to_up.start()
    corner_to_down.start()

    def real_row(v, f, r):
        return sideways(v, left_f[pl.ds(f * TH + r, 1), :], right_f[pl.ds(f * TH + r, 1), :])

    def put(ref, f, q, one, two, which):
        at = pl.ds(pl.multiple_of(q * PAIR, 16), PAIR)
        for e in which:
            ref[e, f, at, :] = jnp.concatenate([one[e], two[e]], axis=0).astype(jnp.bfloat16)

    def own_pair(f, q):
        v = xo[1, f, pl.ds(pl.multiple_of(q * PAIR, 16), PAIR), :].astype(jnp.float32)
        return real_row(v[:TW], f, 2 * q), real_row(v[TW:], f, 2 * q + 1)

    def second_of(f, q):
        v = xo[1, f, pl.ds(pl.multiple_of(q * PAIR + 48, 16), 64), :].astype(jnp.float32)
        return real_row(v[8:], f, 2 * q + 1)

    def build(f, q):
        above = second_of(f, q - 1)
        one, two = own_pair(f, q)
        put(xe, f, q, above, one, (0, 1, 2))
        put(xo, f, q, one, two, (0, 2))

    def block(w, core_slot, core, b):
        base = b * BR
        parts = []
        for a, y, e in TAPS:
            ref = xo if y == 1 else xe
            at = pl.multiple_of(base + (PAIR if y == 2 else 0), 16)
            parts.append(ref[e, a:a + 2, pl.ds(at, BR), :].reshape(MB, CB))
        product = jnp.dot(jnp.concatenate(parts, axis=1), w[...], preferred_element_type=jnp.float32)
        core_out[core_slot, b] = product[:, :CB]
        core(b).start()
        keep[b] = product[:, CB:]

    def core_far(b):
        return remote(core_out.at[0, b], core_in.at[0, b], core_ss.at[0, b], core_rs.at[0, b], mate)

    def core_near(b):
        return remote(core_out.at[1, b], core_in.at[1, b], core_ss.at[1, b], core_rs.at[1, b], mate)

    def cross(b):
        return remote(cross_out.at[b], cross_in.at[b], cross_ss.at[b], cross_rs.at[b], across)

    def pass_on(b):
        core_far(b).wait_recv()
        cross_out[b] = encode(keep[b] + core_in[0, b])
        cross(b).start()

    @pl.loop(0, 8)
    def _(i):
        build(i % 4, 2 + i // 4)

    loads[2].wait()
    loads[3].wait()

    @pl.loop(1, NB - 1)
    def _(b):
        @pl.loop(0, 4)
        def _(f):
            build(f, 2 * b + 2)

            @pl.when(b > 1)
            def _():
                build(f, 2 * b + 1)

        block(wr, 0, core_far, b)

        @pl.when(b > 1)
        def _():
            pass_on(b - 1)

    to_up.wait_recv()
    to_down.wait_recv()
    corner_to_up.wait_recv()
    corner_to_down.wait_recv()

    def corner(ref, f, keep_it):
        pair = jnp.where(keep_it, ref[...].astype(jnp.float32), 0.0)
        return pair[2 * f:2 * f + 1], pair[2 * f + 1:2 * f + 2]

    for f in range(4):
        v = jnp.where(row > 0, halo_a[f].astype(jnp.float32)[8:], 0.0)
        above = sideways(v, *corner(corner_a, f, row > 0))
        one, two = own_pair(f, 0)
        put(xe, f, 0, above, one, (0, 1, 2))
        put(xo, f, 0, one, two, (0, 2))
        build(f, 1)
    block(wr, 0, core_far, 0)
    pass_on(NB - 2)
    for f in range(4):
        build(f, TH // 2 - 1)
        v = jnp.where(row < GY - 1, halo_b[f].astype(jnp.float32)[:TW], 0.0)
        below = sideways(v, *corner(corner_b, f, row < GY - 1))
        put(xe, f, TH // 2, second_of(f, TH // 2 - 1), below, (0, 1, 2))
    block(wr, 0, core_far, NB - 1)
    pass_on(0)
    loads[4].wait()
    loads[5].wait()
    pass_on(NB - 1)

    @pl.loop(0, NB)
    def _(b):
        block(wl, 1, core_near, b)

    def store(b):
        at = pl.ds(pl.multiple_of(b * BR, 16), BR)
        return pltpu.make_async_copy(out_v.at[:, at], out.at[:, at], out_sem.at[b])

    @pl.loop(1, NB + 1)
    def _(i):
        b = jnp.where(i == NB, NB - 1, jnp.where(i == NB - 1, 0, i))
        core_near(b).wait_recv()
        cross(b).wait_recv()
        v = keep[b] + core_in[1, b] + decode(cross_in[b]) + bias[...]
        v = v / (1.0 + jnp.exp(-v))
        out_v[:, pl.ds(pl.multiple_of(b * BR, 16), BR), :] = v.astype(jnp.bfloat16).reshape(2, BR, CB)
        store(b).start()

    for copy in (to_left, to_right, to_up, to_down, corner_to_up, corner_to_down):
        copy.wait_send()

    @pl.loop(0, NB)
    def _(b):
        core_far(b).wait_send()
        core_near(b).wait_send()
        cross(b).wait_send()
        store(b).wait()


def shards(frames, cached, weight, out_bias):
    anywhere = pl.BlockSpec(memory_space=pl.ANY)
    bf16, f32 = jnp.bfloat16, jnp.float32
    out = pl.pallas_call(
        kernel,
        out_shape=jax.ShapeDtypeStruct((2, PIX, CB), bf16),
        in_specs=[anywhere, anywhere, anywhere, pl.BlockSpec(memory_space=pltpu.VMEM)],
        out_specs=anywhere,
        scratch_shapes=[
            pltpu.VMEM((3, 4, PIX + PAIR, CB), bf16),
            pltpu.VMEM((3, 4, PIX, CB), bf16),
            pltpu.VMEM((27 * CB, 2 * CB), bf16),
            pltpu.VMEM((27 * CB, 2 * CB), bf16),
            *[pltpu.VMEM((4 * TH, CB), bf16)] * 4,
            *[pltpu.VMEM((4 * TH, CB), f32)] * 2,
            *[pltpu.VMEM((4, 64, CB), bf16)] * 2,
            *[pltpu.VMEM((16, CB), bf16)] * 4,
            pltpu.VMEM((2, NB, MB, CB), f32),
            pltpu.VMEM((2, NB, MB, CB), f32),
            pltpu.VMEM((NB, MB, CB), f32),
            pltpu.VMEM((NB, MB, CB), bf16),
            pltpu.VMEM((NB, MB, CB), bf16),
            pltpu.VMEM((2, PIX, CB), bf16),
            pltpu.SemaphoreType.DMA((6,)),
            pltpu.SemaphoreType.DMA((6,)),
            pltpu.SemaphoreType.DMA((6,)),
            pltpu.SemaphoreType.DMA((2, NB)),
            pltpu.SemaphoreType.DMA((2, NB)),
            pltpu.SemaphoreType.DMA((NB,)),
            pltpu.SemaphoreType.DMA((NB,)),
            pltpu.SemaphoreType.DMA((NB,)),
        ],
        compiler_params=pltpu.CompilerParams(collective_id=0, has_side_effects=True, vmem_limit_bytes=48 << 20),
        cost_estimate=pl.CostEstimate(flops=2 * 2 * PIX * 27 * CB * 4 * CB, bytes_accessed=7 << 20, transcendentals=2 * PIX * CB),
        name="conv",
    )(
        cached.reshape(2, PIX, CB),
        frames.reshape(2, PIX, CB),
        weight.reshape(27 * CB, 4 * CB),
        out_bias.reshape(1, CB),
    )
    return out.reshape(2, 1, TH, TW, CB)


def solution(mesh):
    in_specs = (
        P(None, "tile", None, None, "ch"),
        P(None, "tile", None, None, "ch"),
        P(None, None, None, "ch", None),
        P("ch"),
    )
    out_specs = P(None, "tile", None, None, "ch")
    return jax.shard_map(shards, mesh=mesh, in_specs=in_specs, out_specs=out_specs, check_vma=False)
```

```python
import jax
import jax.numpy as jnp
from jax import lax
from jax.experimental import pallas as pl
from jax.experimental.pallas import tpu as pltpu
from jax.sharding import PartitionSpec as P

GX = 8
GY = 8
TH = 32
TW = 56
CB = 128
PIX = TH * TW
PAIR = 2 * TW
NP = TH // 2
SCALE = 2.0**20
MESH = pl.DeviceIdType.MESH
TAPS = [(a, b, e) for a in range(3) for b in range(3) for e in range(3)]
INNER = [(16, 32), (64, 32)]
RIM = [(0, 16), (48, 16), (96, 16)]
WHOLE = [(0, PAIR)]
INNER_ROWS, RIM_ROWS, END_ROWS = 2 * 64, 2 * 48, 2 * PAIR
MIDDLE = NP - 2
RIM_AT = MIDDLE * INNER_ROWS
END_AT = RIM_AT + MIDDLE * RIM_ROWS
ROWS = END_AT + 2 * END_ROWS
FIRST = [(0, 2), (2, 2), (4, 5), (9, 5)]
HALF = MIDDLE // 2


def encode(v):
    s = v * SCALE
    return ((s * s) * (s * jnp.abs(s))).astype(jnp.bfloat16)


def decode(w):
    w = w.astype(jnp.float32)
    root = jnp.sqrt(jnp.sqrt(jnp.abs(w))) * (1.0 / SCALE)
    return jnp.where(w < 0, -root, root)


def sideways(v):
    return pltpu.roll(v, 1, 0), v, pltpu.roll(v, TW - 1, 0)


def ends(moved, left, right):
    m, v, p = moved
    lane = lax.broadcasted_iota(jnp.int32, (8, CB), 0)
    m = jnp.concatenate([jnp.where(lane == 0, left, m[:8]), m[8:]], axis=0)
    p = jnp.concatenate([p[:-8], jnp.where(lane == 7, right, p[-8:])], axis=0)
    return m, v, p


def aligned(i):
    return i if isinstance(i, int) else pl.multiple_of(i, 16)


def kernel(cached, frames, weight, bias_in, out, xe, xo, w, bias, edge_l, edge_r, halo_l, halo_r, left_f, right_f, halo_a, halo_b,
           corner_up, corner_dn, corner_a, corner_b, core_out, core_in, keep, cross_out, cross_in,
           in_sem, halo_ss, halo_rs, far_ss, far_rs, near_ss, near_rs, cross_ss, cross_rs):
    ch = lax.axis_index("ch")
    tile = lax.axis_index("tile")
    h, c = ch // 2, ch % 2
    row, col = tile // GX, tile % GX
    left = (ch, row * GX + (col + GX - 1) % GX)
    right = (ch, row * GX + (col + 1) % GX)
    up = (ch, ((row + GY - 1) % GY) * GX + col)
    down = (ch, ((row + 1) % GY) * GX + col)
    mate = (h * 2 + (1 - c), tile)
    across = ((1 - h) * 2 + c, tile)

    loads = [
        pltpu.make_async_copy(cached, xo.at[1, pl.ds(0, 2)], in_sem.at[0]),
        pltpu.make_async_copy(frames, xo.at[1, pl.ds(2, 2)], in_sem.at[1]),
    ]
    for i, group in enumerate([(1 - h) * 2 + 1 - c, (1 - h) * 2 + c, h * 2 + 1 - c, ch]):
        loads.append(pltpu.make_async_copy(
            weight.at[:, pl.ds(pl.multiple_of(group * CB, CB), CB)], w.at[:, pl.ds(i * CB, CB)], in_sem.at[2 + i]))
    loads.append(pltpu.make_async_copy(bias_in, bias, in_sem.at[6]))
    for load in loads:
        load.start()

    barrier = pltpu.get_barrier_semaphore()
    for device in (left, right, up, down, mate, across):
        pl.semaphore_signal(barrier, inc=1, device_id=device, device_id_type=MESH)
    loads[0].wait()
    loads[1].wait()

    def put(ref, f, q, one, two, which):
        at = pl.ds(aligned(q * PAIR), PAIR)
        for e in which:
            ref[e, f, at, :] = jnp.concatenate([one[e], two[e]], axis=0).astype(jnp.bfloat16)

    def own_pair(f, q):
        v = xo[1, f, pl.ds(aligned(q * PAIR), PAIR), :].astype(jnp.float32)
        return sideways(v[:TW]), sideways(v[TW:])

    def second_of(f, q):
        return sideways(xo[1, f, pl.ds(aligned(q * PAIR + 48), 64), :].astype(jnp.float32)[8:])

    def build(f, q):
        above = second_of(f, q - 1)
        one, two = own_pair(f, q)
        put(xe, f, q, above, one, (0, 1, 2))
        put(xo, f, q, one, two, (0, 2))

    def build_all(q0, q1):
        @pl.loop(0, 4 * (q1 - q0))
        def _(i):
            build(i % 4, q0 + i // 4)

    def remote(src, dst, ss, rs, device):
        return pltpu.make_async_remote_copy(src_ref=src, dst_ref=dst, send_sem=ss, recv_sem=rs, device_id=device, device_id_type=MESH)

    def far_core(i, at, n):
        at = pl.ds(aligned(at), n)
        return remote(core_out.at[0, at], core_in.at[0, at], far_ss.at[i], far_rs.at[i], mate)

    def near_core(i, at, n):
        at = pl.ds(aligned(at), n)
        return remote(core_out.at[1, at], core_in.at[1, at], near_ss.at[i], near_rs.at[i], mate)

    def cross(i, at, n):
        at = pl.ds(aligned(at), n)
        return remote(cross_out.at[at], cross_in.at[at], cross_ss.at[i], cross_rs.at[i], across)

    def pass_on(i, at, n):
        far_core(i, at, n).wait_recv()
        rows = pl.ds(aligned(at), n)
        cross_out[rows, :] = encode(keep[0, rows, :] + core_in[0, rows, :])
        cross(i, at, n).start()

    def product(qs, segments, sides, at):
        columns = []
        for a, y, e in TAPS:
            ref = xo if y == 1 else xe
            pieces = []
            for q in qs:
                for start, n in segments:
                    rows = pl.ds(aligned(q * PAIR + start + (PAIR if y == 2 else 0)), n)
                    pieces.append(ref[e, a:a + 2, rows, :].reshape(2 * n, CB))
            columns.append(jnp.concatenate(pieces, axis=0) if len(pieces) > 1 else pieces[0])
        first = sides[0] * 2 * CB
        sums = jnp.dot(
            jnp.concatenate(columns, axis=1), w[:, first:first + len(sides) * 2 * CB], preferred_element_type=jnp.float32)
        rows = pl.ds(aligned(at), sums.shape[0])
        for k, side in enumerate(sides):
            core_out[side, rows, :] = sums[:, 2 * k * CB:(2 * k + 1) * CB]
            keep[side, rows, :] = sums[:, (2 * k + 1) * CB:(2 * k + 2) * CB]

    def inner(i0, n, sides):
        product([1 + i0 + k for k in range(n)], INNER, sides, i0 * INNER_ROWS)

    inner_rows = [(i, i0 * INNER_ROWS, n * INNER_ROWS) for i, (i0, n) in enumerate(FIRST)]
    end_rows = (6, END_AT, 2 * END_ROWS)

    def rim_rows(i):
        return 4 + i, RIM_AT + i * HALF * RIM_ROWS, HALF * RIM_ROWS

    lane = lax.broadcasted_iota(jnp.int32, (8, CB), 0)

    @pl.loop(0, 4)
    def _(f):
        for g in range(2):
            acc_l = [jnp.zeros((8, CB), jnp.float32)] * 2
            acc_r = [jnp.zeros((8, CB), jnp.float32)] * 2
            for q in range(8):
                at = (g * 8 + q) * PAIR
                start = xo[1, f, at:at + 16, :].astype(jnp.float32)
                middle = xo[1, f, at + 48:at + 64, :].astype(jnp.float32)
                last = xo[1, f, at + 96:at + 112, :].astype(jnp.float32)
                k, d = (2 * q) // 8, (2 * q) % 8
                acc_l[k] = jnp.where(lane == d, start[0:1], acc_l[k])
                acc_r[k] = jnp.where(lane == d, middle[7:8], acc_r[k])
                acc_l[k] = jnp.where(lane == d + 1, middle[8:9], acc_l[k])
                acc_r[k] = jnp.where(lane == d + 1, last[15:16], acc_r[k])
            at = pl.ds(pl.multiple_of(f * TH + g * 16, 16), 16)
            edge_l[at, :] = jnp.concatenate(acc_l, axis=0).astype(jnp.bfloat16)
            edge_r[at, :] = jnp.concatenate(acc_r, axis=0).astype(jnp.bfloat16)

    build_all(1, 4)
    loads[2].wait()
    loads[3].wait()
    inner(*FIRST[0], [0])
    pl.semaphore_wait(barrier, 6)
    far_core(*inner_rows[0]).start()

    to_left = remote(edge_l, halo_r, halo_ss.at[0], halo_rs.at[0], left)
    to_right = remote(edge_r, halo_l, halo_ss.at[1], halo_rs.at[1], right)
    to_up = remote(xo.at[1, :, pl.ds(0, 64)], halo_b, halo_ss.at[2], halo_rs.at[2], up)
    to_down = remote(xo.at[1, :, pl.ds(PIX - 64, 64)], halo_a, halo_ss.at[3], halo_rs.at[3], down)
    to_left.start()
    to_right.start()
    to_up.start()
    to_down.start()

    build_all(4, 6)
    inner(*FIRST[1], [0])
    far_core(*inner_rows[1]).start()
    build_all(6, 11)
    pass_on(*inner_rows[0])
    inner(*FIRST[2], [0])
    far_core(*inner_rows[2]).start()
    pass_on(*inner_rows[1])
    build_all(11, NP)
    inner(*FIRST[3], [0])
    far_core(*inner_rows[3]).start()
    pass_on(*inner_rows[2])

    to_left.wait_recv()
    to_right.wait_recv()
    left_f[...] = jnp.where(col > 0, halo_l[...].astype(jnp.float32), 0.0)
    right_f[...] = jnp.where(col < GX - 1, halo_r[...].astype(jnp.float32), 0.0)

    for ref, r in ((corner_up, 0), (corner_dn, TH - 1)):
        pieces = []
        for f in range(4):
            pieces += [left_f[f * TH + r:f * TH + r + 1, :], right_f[f * TH + r:f * TH + r + 1, :]]
        ref[...] = jnp.concatenate(pieces + [jnp.zeros((8, CB), jnp.float32)], axis=0).astype(jnp.bfloat16)
    corner_to_up = remote(corner_up, corner_b, halo_ss.at[4], halo_rs.at[4], up)
    corner_to_down = remote(corner_dn, corner_a, halo_ss.at[5], halo_rs.at[5], down)
    corner_to_up.start()
    corner_to_down.start()

    place = lax.broadcasted_iota(jnp.int32, (16, CB), 0)

    def side_pixels(f, r):
        at = pl.ds(f * TH + r, 1)
        return left_f[at, :], right_f[at, :]

    @pl.loop(0, 4 * (NP - 1))
    def _(i):
        f, q = i % 4, 1 + i // 4
        for ref, r in ((xe, 2 * q - 1), (xo, 2 * q)):
            one, two = side_pixels(f, r), side_pixels(f, r + 1)
            for e, start, k, pixel in ((0, 0, 0, one[0]), (0, 48, 8, two[0]), (2, 48, 7, one[1]), (2, 96, 15, two[1])):
                at = pl.ds(aligned(q * PAIR + start), 16)
                ref[e, f, at, :] = jnp.where(place == k, pixel, ref[e, f, at, :].astype(jnp.float32)).astype(jnp.bfloat16)

    pass_on(*inner_rows[3])
    loads[4].wait()
    loads[5].wait()

    @pl.loop(0, 2)
    def _(i):
        product([1 + i * HALF + k for k in range(HALF)], RIM, [0, 1], RIM_AT + i * HALF * RIM_ROWS)
        far_core(*rim_rows(i)).start()
        near_core(2 + i, *rim_rows(i)[1:]).start()

        @pl.when(i == 1)
        def _():
            pass_on(*rim_rows(0))

    to_up.wait_recv()
    to_down.wait_recv()
    corner_to_up.wait_recv()
    corner_to_down.wait_recv()

    def corner(ref, f, inside):
        pair = jnp.where(inside, ref[...].astype(jnp.float32), 0.0)
        return pair[2 * f:2 * f + 1], pair[2 * f + 1:2 * f + 2]

    for f in range(4):
        v = jnp.where(row > 0, halo_a[f].astype(jnp.float32)[8:], 0.0)
        above = ends(sideways(v), *corner(corner_a, f, row > 0))
        one, two = own_pair(f, 0)
        one, two = ends(one, *side_pixels(f, 0)), ends(two, *side_pixels(f, 1))
        put(xe, f, 0, above, one, (0, 1, 2))
        put(xo, f, 0, one, two, (0, 2))
        v = jnp.where(row < GY - 1, halo_b[f].astype(jnp.float32)[:TW], 0.0)
        below = ends(sideways(v), *corner(corner_b, f, row < GY - 1))
        put(xe, f, NP, ends(second_of(f, NP - 1), *side_pixels(f, TH - 1)), below, (0, 1, 2))
    pass_on(*rim_rows(1))
    product([0, NP - 1], WHOLE, [0, 1], END_AT)
    far_core(*end_rows).start()
    near_core(4, *end_rows[1:]).start()

    @pl.loop(0, 2)
    def _(i):
        inner(i * HALF, HALF, [1])
        near_core(i, i * HALF * INNER_ROWS, HALF * INNER_ROWS).start()

        @pl.when(i == 0)
        def _():
            pass_on(*end_rows)

    loads[6].wait()

    def finish(q, segments, at, n):
        rows = pl.ds(aligned(at), n)
        v = keep[1, rows, :] + core_in[1, rows, :] + decode(cross_in[rows, :]) + bias[...]
        v = (v / (1.0 + jnp.exp(-v))).astype(jnp.bfloat16)
        at = 0
        for start, k in segments:
            for f in range(2):
                out[f, pl.ds(aligned(q * PAIR + start), k), :] = v[at:at + k]
                at += k

    for i in range(2):
        near_core(i, i * HALF * INNER_ROWS, HALF * INNER_ROWS).wait_recv()
    for i, (i0, n) in enumerate(FIRST):
        cross(*inner_rows[i]).wait_recv()

        @pl.loop(i0, i0 + n)
        def _(k):
            finish(1 + k, INNER, k * INNER_ROWS, INNER_ROWS)

    for i in range(2):
        near_core(2 + i, *rim_rows(i)[1:]).wait_recv()
        cross(*rim_rows(i)).wait_recv()

        @pl.loop(i * HALF, (i + 1) * HALF)
        def _(k):
            finish(1 + k, RIM, RIM_AT + k * RIM_ROWS, RIM_ROWS)

    near_core(4, *end_rows[1:]).wait_recv()
    for copy in (to_left, to_right, to_up, to_down, corner_to_up, corner_to_down):
        copy.wait_send()
    for i in range(2):
        near_core(i, i * HALF * INNER_ROWS, HALF * INNER_ROWS).wait_send()
        near_core(2 + i, *rim_rows(i)[1:]).wait_send()
    near_core(4, *end_rows[1:]).wait_send()
    for rows in (*inner_rows, rim_rows(0), rim_rows(1), end_rows):
        far_core(*rows).wait_send()
    cross(*end_rows).wait_recv()
    finish(0, WHOLE, END_AT, END_ROWS)
    finish(NP - 1, WHOLE, END_AT + END_ROWS, END_ROWS)
    for rows in (*inner_rows, rim_rows(0), rim_rows(1), end_rows):
        cross(*rows).wait_send()


def shards(frames, cached, weight, out_bias):
    anywhere = pl.BlockSpec(memory_space=pl.ANY)
    bf16, f32 = jnp.bfloat16, jnp.float32
    operands = (
        cached.reshape(2, PIX, CB),
        frames.reshape(2, PIX, CB),
        weight.reshape(27 * CB, 4 * CB),
        out_bias.reshape(1, CB),
    )
    out = pl.pallas_call(
        kernel,
        out_shape=jax.ShapeDtypeStruct((2, PIX, CB), bf16),
        in_specs=[anywhere] * 4,
        out_specs=pl.BlockSpec(memory_space=pltpu.VMEM),
        scratch_shapes=[
            pltpu.VMEM((3, 4, PIX + PAIR, CB), bf16),
            pltpu.VMEM((3, 4, PIX, CB), bf16),
            pltpu.VMEM((27 * CB, 4 * CB), bf16),
            pltpu.VMEM((1, CB), f32),
            *[pltpu.VMEM((4 * TH, CB), bf16)] * 4,
            *[pltpu.VMEM((4 * TH, CB), f32)] * 2,
            *[pltpu.VMEM((4, 64, CB), bf16)] * 2,
            *[pltpu.VMEM((16, CB), bf16)] * 4,
            *[pltpu.VMEM((2, ROWS, CB), f32)] * 3,
            *[pltpu.VMEM((ROWS, CB), bf16)] * 2,
            *[pltpu.SemaphoreType.DMA((7,))] * 1,
            *[pltpu.SemaphoreType.DMA((6,))] * 2,
            *[pltpu.SemaphoreType.DMA((7,))] * 2,
            *[pltpu.SemaphoreType.DMA((5,))] * 2,
            *[pltpu.SemaphoreType.DMA((7,))] * 2,
        ],
        compiler_params=pltpu.CompilerParams(collective_id=0, has_side_effects=True, vmem_limit_bytes=48 << 20),
        cost_estimate=pl.CostEstimate(flops=2 * 2 * PIX * 27 * CB * 4 * CB, bytes_accessed=7 << 20, transcendentals=2 * PIX * CB),
        name="conv",
    )(*[pltpu.with_memory_space_constraint(x, pltpu.HBM) for x in operands])
    return out.reshape(2, 1, TH, TW, CB)


def solution(mesh):
    in_specs = (
        P(None, "tile", None, None, "ch"),
        P(None, "tile", None, None, "ch"),
        P(None, None, None, "ch", None),
        P("ch"),
    )
    out_specs = P(None, "tile", None, None, "ch")
    return jax.shard_map(shards, mesh=mesh, in_specs=in_specs, out_specs=out_specs, check_vma=False)
```

```python
import jax
import jax.numpy as jnp
from jax import lax
from jax.experimental import pallas as pl
from jax.experimental.pallas import tpu as pltpu
from jax.sharding import PartitionSpec as P

GX = 8
GY = 8
TH = 32
TW = 56
CB = 128
PIX = TH * TW
PAIR = 2 * TW
NP = TH // 2
SLOTS = TW // 8
SLOT = 16
WIDE = (SLOTS + 2) * SLOT
FRAME = 8 + (TH + 2) * TW + 8
SIDE = TH + 16
SCALE = 2.0**20
MESH = pl.DeviceIdType.MESH
TAPS = [(a, b, e) for a in range(3) for b in range(3) for e in range(3)]
INNER = [(1, 5)]
RIM = [(0, 1), (6, 1)]
WHOLE = [(0, 7)]
INNER_ROWS, RIM_ROWS, END_ROWS = 2 * 5 * SLOT, 2 * 2 * SLOT, 2 * PAIR
MIDDLE = NP - 2
RIM_AT = MIDDLE * INNER_ROWS
END_AT = RIM_AT + MIDDLE * RIM_ROWS
ROWS = END_AT + 2 * END_ROWS
BLOCKS = 7
BLOCK = MIDDLE // BLOCKS
BLOCK_ROWS = BLOCK * INNER_ROWS
HALF = MIDDLE // 2
HALF_ROWS = HALF * RIM_ROWS
PARTS = BLOCKS + 4


def encode(v):
    s = v * SCALE
    return ((s * s) * (s * jnp.abs(s))).astype(jnp.bfloat16)


def decode(w):
    w = w.astype(jnp.float32)
    root = jnp.sqrt(jnp.sqrt(jnp.abs(w))) * (1.0 / SCALE)
    return jnp.where(w < 0, -root, root)


def kernel(cached, frames, weight, bias_in, out, xin, xf, xe, xo, w, bias, edge_l, edge_r, halo_l, halo_r, left_f, right_f,
           halo_a, halo_b, corner_up, corner_dn, corner_a, corner_b, core_out, core_in, keep, cross_out, cross_in, out_f,
           in_sem, halo_ss, halo_rs, core_ss, core_rs, cross_ss, cross_rs):
    ch = lax.axis_index("ch")
    tile = lax.axis_index("tile")
    h, c = ch // 2, ch % 2
    row, col = tile // GX, tile % GX
    left = (ch, row * GX + (col + GX - 1) % GX)
    right = (ch, row * GX + (col + 1) % GX)
    up = (ch, ((row + GY - 1) % GY) * GX + col)
    down = (ch, ((row + 1) % GY) * GX + col)
    mate = (h * 2 + (1 - c), tile)
    across = ((1 - h) * 2 + c, tile)

    loads = [
        pltpu.make_async_copy(cached, xin.at[pl.ds(0, 2)], in_sem.at[0]),
        pltpu.make_async_copy(frames, xin.at[pl.ds(2, 2)], in_sem.at[1]),
    ]
    for i, group in enumerate([(1 - h) * 2 + 1 - c, (1 - h) * 2 + c, h * 2 + 1 - c, ch]):
        loads.append(pltpu.make_async_copy(
            weight.at[:, pl.ds(pl.multiple_of(group * CB, CB), CB)], w.at[i // 2, :, pl.ds(i % 2 * CB, CB)], in_sem.at[2 + i]))
    loads.append(pltpu.make_async_copy(bias_in, bias, in_sem.at[6]))
    for load in loads:
        load.start()

    barrier = pltpu.get_barrier_semaphore()
    for device in (left, right, up, down, mate, across):
        pl.semaphore_signal(barrier, inc=1, device_id=device, device_id_type=MESH)

    def remote(src, dst, ss, rs, device):
        return pltpu.make_async_remote_copy(src_ref=src, dst_ref=dst, send_sem=ss, recv_sem=rs, device_id=device, device_id_type=MESH)

    def block(i):
        return i, i * BLOCK_ROWS, BLOCK_ROWS

    def half(i):
        return BLOCKS + i, RIM_AT + i * HALF_ROWS, HALF_ROWS

    def end(i):
        return BLOCKS + 2 + i, END_AT + i * END_ROWS, END_ROWS

    def rows_of(at, n):
        return pl.ds(at if isinstance(at, int) else pl.multiple_of(at, 16), n)

    def core(side, part):
        i, at, n = part
        rows = rows_of(at, n)
        return remote(core_out.at[side, rows], core_in.at[side, rows], core_ss.at[side, i], core_rs.at[side, i], mate)

    def cross(part):
        i, at, n = part
        rows = rows_of(at, n)
        return remote(cross_out.at[rows], cross_in.at[rows], cross_ss.at[i], cross_rs.at[i], across)

    def pass_on(part):
        core(0, part).wait_recv()
        rows = rows_of(*part[1:])
        cross_out[rows, :] = encode(keep[0, rows, :] + core_in[0, rows, :])
        cross(part).start()

    def place_of(f, r):
        return f * FRAME + 8 + (r + 1) * TW

    def build(ref, f, q, r):
        for k in range(SLOTS):
            v = xf[pl.ds(place_of(f, r) + k, SLOT, stride=SLOTS), :]
            ref[f, q, (k + 1) * SLOT:(k + 2) * SLOT, :] = v.astype(jnp.bfloat16)

    spot = lax.broadcasted_iota(jnp.int32, (SLOT, CB), 0)

    def build_sides(ref, f, q, r):
        for side, k, slot in ((left_f, -1, 0), (right_f, SLOTS, SLOTS + 1)):
            v = xf[pl.ds(place_of(f, r) + k, SLOT, stride=SLOTS), :]
            at = 0 if k < 0 else 7
            for j in range(2):
                v = jnp.where(spot == at + 8 * j, side[pl.ds(f * SIDE + 8 + r + j, 1), :], v)
            ref[f, q, slot * SLOT:(slot + 1) * SLOT, :] = v.astype(jnp.bfloat16)

    def build_all(q0, q1):
        @pl.loop(q0, q1)
        def _(q):
            for f in range(4):
                build(xo, f, q, 2 * q)
                build(xe, f, q, 2 * q - 1)

    def product(groups, slots, side, at):
        columns = []
        for a, y, e in TAPS:
            pieces = []
            for q, n in groups:
                for first, count in slots:
                    ref, q_at = (xo, q) if y == 1 else (xe, q + y // 2)
                    v = ref[a:a + 2, pl.ds(q_at, n), (first + e) * SLOT:(first + e + count) * SLOT, :]
                    pieces.append(v.reshape(2 * n * count * SLOT, CB))
            columns.append(jnp.concatenate(pieces, axis=0) if len(pieces) > 1 else pieces[0])
        sums = jnp.dot(jnp.concatenate(columns, axis=1), w[side], preferred_element_type=jnp.float32)
        rows = rows_of(at, sums.shape[0])
        core_out[side, rows, :] = sums[:, :CB]
        keep[side, rows, :] = sums[:, CB:]

    loads[0].wait()
    loads[1].wait()

    @pl.loop(0, NP)
    def _(q):
        for f in range(4):
            v = xin[f, pl.ds(pl.multiple_of(q * PAIR, 16), PAIR), :]
            xf[pl.ds(pl.multiple_of(place_of(f, 2 * q), 8), PAIR), :] = v.astype(jnp.float32)

    for f in range(4):
        at = f * TH
        edge_l[at:at + TH, :] = xf[pl.ds(place_of(f, 0), TH, stride=TW), :].astype(jnp.bfloat16)
        edge_r[at:at + TH, :] = xf[pl.ds(place_of(f, 0) + TW - 1, TH, stride=TW), :].astype(jnp.bfloat16)

    build_all(1, 4)
    loads[2].wait()
    loads[3].wait()
    to_left = remote(edge_l, halo_r, halo_ss.at[0], halo_rs.at[0], left)
    to_right = remote(edge_r, halo_l, halo_ss.at[1], halo_rs.at[1], right)
    to_up = remote(xin.at[:, pl.ds(0, 64)], halo_b, halo_ss.at[2], halo_rs.at[2], up)
    to_down = remote(xin.at[:, pl.ds(PIX - 64, 64)], halo_a, halo_ss.at[3], halo_rs.at[3], down)
    halos = (to_left, to_right, to_up, to_down)

    @pl.loop(0, 2 * BLOCKS)
    def _(j):
        side, b = j // BLOCKS, j % BLOCKS

        @pl.when(j == BLOCKS)
        def _():
            loads[4].wait()
            loads[5].wait()

        product([(1 + b * BLOCK, BLOCK)], INNER, side, b * BLOCK_ROWS)

        @pl.when(j == 0)
        def _():
            pl.semaphore_wait(barrier, 6)
            core(side, block(b)).start()
            for halo in halos:
                halo.start()

        @pl.when(j > 0)
        def _():
            core(side, block(b)).start()

        @pl.when(j < BLOCKS - 1)
        def _():
            build_all(2 + (b + 1) * BLOCK, 2 + (b + 2) * BLOCK)

        @pl.when((j > 0) & (j <= BLOCKS))
        def _():
            pass_on(block(j - 1))

    to_left.wait_recv()
    to_right.wait_recv()
    for f in range(4):
        at, to = f * TH, f * SIDE + 8
        left_f[to:to + TH, :] = jnp.where(col > 0, halo_l[at:at + TH, :].astype(jnp.float32), 0.0)
        right_f[to:to + TH, :] = jnp.where(col < GX - 1, halo_r[at:at + TH, :].astype(jnp.float32), 0.0)

    for ref, r in ((corner_up, 0), (corner_dn, TH - 1)):
        pieces = []
        for f in range(4):
            at = f * SIDE + 8 + r
            pieces += [left_f[at:at + 1, :], right_f[at:at + 1, :]]
        ref[...] = jnp.concatenate(pieces + [jnp.zeros((8, CB), jnp.float32)], axis=0).astype(jnp.bfloat16)
    corner_to_up = remote(corner_up, corner_b, halo_ss.at[4], halo_rs.at[4], up)
    corner_to_down = remote(corner_dn, corner_a, halo_ss.at[5], halo_rs.at[5], down)
    corners = (corner_to_up, corner_to_down)
    for corner in corners:
        corner.start()

    @pl.loop(1, NP)
    def _(q):
        for f in range(4):
            build_sides(xo, f, q, 2 * q)
            build_sides(xe, f, q, 2 * q - 1)

    def rim(side):
        @pl.loop(0, 2)
        def _(i):
            product([(1 + i * HALF, HALF)], RIM, side, RIM_AT + i * HALF_ROWS)
            core(side, half(i)).start()

    def both_ends(side):
        product([(0, 1), (NP - 1, 1)], WHOLE, side, END_AT)
        core(side, end(0)).start()
        core(side, end(1)).start()

    rim(0)
    to_up.wait_recv()
    to_down.wait_recv()
    for corner in corners:
        corner.wait_recv()
    above = jnp.where(row > 0, corner_a[...].astype(jnp.float32), 0.0)
    below = jnp.where(row < GY - 1, corner_b[...].astype(jnp.float32), 0.0)
    for f in range(4):
        xf[pl.ds(place_of(f, -1), TW), :] = jnp.where(row > 0, halo_a[f].astype(jnp.float32)[8:], 0.0)
        xf[pl.ds(place_of(f, TH), TW), :] = jnp.where(row < GY - 1, halo_b[f].astype(jnp.float32)[:TW], 0.0)
        at = f * SIDE + 8
        left_f[at - 1:at, :] = above[2 * f:2 * f + 1]
        right_f[at - 1:at, :] = above[2 * f + 1:2 * f + 2]
        left_f[at + TH:at + TH + 1, :] = below[2 * f:2 * f + 1]
        right_f[at + TH:at + TH + 1, :] = below[2 * f + 1:2 * f + 2]
    for f in range(4):
        for ref, q, r in ((xo, 0, 0), (xe, 0, -1), (xe, NP, TH - 1)):
            build(ref, f, q, r)
            build_sides(ref, f, q, r)

    both_ends(0)
    pass_on(half(0))
    pass_on(half(1))
    rim(1)
    pass_on(end(0))
    pass_on(end(1))
    both_ends(1)
    loads[6].wait()

    def finished(at, n):
        rows = pl.ds(at, n)
        v = keep[1, rows, :] + core_in[1, rows, :] + decode(cross_in[rows, :]) + bias[...]
        return v / (1.0 + jnp.exp(-v))

    def spread(v, f, q, k):
        out_f[pl.ds(f * PIX + q * PAIR + k, SLOT, stride=SLOTS), :] = v

    def settle(f, q):
        at = pl.multiple_of(q * PAIR, 16)
        out[f, pl.ds(at, PAIR), :] = out_f[pl.ds(pl.multiple_of(f * PIX + at, 16), PAIR), :].astype(jnp.bfloat16)

    @pl.loop(0, BLOCKS)
    def _(b):
        core(1, block(b)).wait_recv()
        cross(block(b)).wait_recv()
        v = finished(pl.multiple_of(b * BLOCK_ROWS, 16), BLOCK_ROWS)
        for f in range(2):
            for p in range(BLOCK):
                for k in range(5):
                    at = ((f * BLOCK + p) * 5 + k) * SLOT
                    spread(v[at:at + SLOT], f, 1 + b * BLOCK + p, 1 + k)

    @pl.loop(0, 2)
    def _(i):
        core(1, half(i)).wait_recv()
        cross(half(i)).wait_recv()
        v = finished(pl.multiple_of(RIM_AT + i * HALF_ROWS, 16), HALF_ROWS)
        for s, k in enumerate((0, 6)):
            for f in range(2):
                for p in range(HALF):
                    at = ((s * 2 + f) * HALF + p) * SLOT
                    spread(v[at:at + SLOT], f, 1 + i * HALF + p, k)

    @pl.loop(1, NP - 1)
    def _(q):
        for f in range(2):
            settle(f, q)

    for copy in halos + corners:
        copy.wait_send()

    @pl.loop(0, 2)
    def _(i):
        core(1, end(i)).wait_recv()
        cross(end(i)).wait_recv()
        v = finished(pl.multiple_of(END_AT + i * END_ROWS, 16), END_ROWS)
        q = i * (NP - 1)
        for f in range(2):
            for k in range(SLOTS):
                at = (f * SLOTS + k) * SLOT
                spread(v[at:at + SLOT], f, q, k)
            settle(f, q)

    def sent(part):
        core(0, part).wait_send()
        core(1, part).wait_send()
        cross(part).wait_send()

    @pl.loop(0, BLOCKS)
    def _(b):
        sent(block(b))

    for i in range(2):
        sent(half(i))
        sent(end(i))


def shards(frames, cached, weight, out_bias):
    bf16, f32 = jnp.bfloat16, jnp.float32
    operands = (
        cached.reshape(2, PIX, CB),
        frames.reshape(2, PIX, CB),
        weight.reshape(27 * CB, 4 * CB),
        out_bias.reshape(1, CB),
    )
    out = pl.pallas_call(
        kernel,
        out_shape=jax.ShapeDtypeStruct((2, PIX, CB), bf16),
        in_specs=[pl.BlockSpec(memory_space=pl.ANY)] * 4,
        out_specs=pl.BlockSpec(memory_space=pltpu.VMEM),
        scratch_shapes=[
            pltpu.VMEM((4, PIX, CB), bf16),
            pltpu.VMEM((4 * FRAME, CB), f32),
            pltpu.VMEM((4, NP + 1, WIDE, CB), bf16),
            pltpu.VMEM((4, NP, WIDE, CB), bf16),
            pltpu.VMEM((2, 27 * CB, 2 * CB), bf16),
            pltpu.VMEM((1, CB), f32),
            *[pltpu.VMEM((4 * TH, CB), bf16)] * 4,
            *[pltpu.VMEM((4 * SIDE, CB), f32)] * 2,
            *[pltpu.VMEM((4, 64, CB), bf16)] * 2,
            *[pltpu.VMEM((16, CB), bf16)] * 4,
            *[pltpu.VMEM((2, ROWS, CB), f32)] * 3,
            *[pltpu.VMEM((ROWS, CB), bf16)] * 2,
            pltpu.VMEM((2 * PIX, CB), f32),
            pltpu.SemaphoreType.DMA((7,)),
            *[pltpu.SemaphoreType.DMA((6,))] * 2,
            *[pltpu.SemaphoreType.DMA((2, PARTS))] * 2,
            *[pltpu.SemaphoreType.DMA((PARTS,))] * 2,
        ],
        compiler_params=pltpu.CompilerParams(collective_id=0, has_side_effects=True, vmem_limit_bytes=48 << 20),
        cost_estimate=pl.CostEstimate(flops=2 * 2 * PIX * 27 * CB * 4 * CB, bytes_accessed=7 << 20, transcendentals=2 * PIX * CB),
        name="conv",
    )(*[pltpu.with_memory_space_constraint(x, pltpu.HBM) for x in operands])
    return out.reshape(2, 1, TH, TW, CB)


def solution(mesh):
    in_specs = (
        P(None, "tile", None, None, "ch"),
        P(None, "tile", None, None, "ch"),
        P(None, None, None, "ch", None),
        P("ch"),
    )
    out_specs = P(None, "tile", None, None, "ch")
    return jax.shard_map(shards, mesh=mesh, in_specs=in_specs, out_specs=out_specs, check_vma=False)
```

```python
import jax
import jax.numpy as jnp
from jax import lax
from jax.experimental import pallas as pl
from jax.experimental.pallas import tpu as pltpu
from jax.sharding import PartitionSpec as P

GX = 8
GY = 8
TH = 32
TW = 56
CB = 128
PIX = TH * TW
PAIR = 2 * TW
NP = TH // 2
SLOTS = TW // 8
SLOT = 16
WIDE = (SLOTS + 2) * SLOT
FRAME = 8 + (TH + 2) * TW + 8
SIDE = TH + 16
SCALE = 2.0**20
MESH = pl.DeviceIdType.MESH
TAPS = [(a, b, e) for a in range(3) for b in range(3) for e in range(3)]
INNER = [(1, 5)]
RIM = [(0, 1), (6, 1)]
WHOLE = [(0, 7)]
INNER_ROWS, RIM_ROWS, END_ROWS = 2 * 5 * SLOT, 2 * 2 * SLOT, 2 * PAIR
MIDDLE = NP - 2
RIM_AT = MIDDLE * INNER_ROWS
END_AT = RIM_AT + MIDDLE * RIM_ROWS
ROWS = END_AT + 2 * END_ROWS
BLOCKS = 7
HALO_AT = 5
BLOCK = MIDDLE // BLOCKS
BLOCK_ROWS = BLOCK * INNER_ROWS
HALF = MIDDLE // 2
HALF_ROWS = HALF * RIM_ROWS
PARTS = BLOCKS + 4


def encode(v):
    s = v * SCALE
    return ((s * s) * (s * jnp.abs(s))).astype(jnp.bfloat16)


def decode(w):
    w = w.astype(jnp.float32)
    root = jnp.sqrt(jnp.sqrt(jnp.abs(w))) * (1.0 / SCALE)
    return jnp.where(w < 0, -root, root)


def kernel(cached, frames, weight, bias_in, out, xin, xf, xe, xo, w, bias, edge_l, edge_r, halo_l, halo_r, left_f, right_f,
           halo_a, halo_b, corner_up, corner_dn, corner_a, corner_b, core_out, core_in, keep, cross_out, cross_in, out_f,
           in_sem, halo_ss, halo_rs, core_ss, core_rs, cross_ss, cross_rs, ready):
    ch = lax.axis_index("ch")
    tile = lax.axis_index("tile")
    h, c = ch // 2, ch % 2
    row, col = tile // GX, tile % GX
    left = (ch, row * GX + (col + GX - 1) % GX)
    right = (ch, row * GX + (col + 1) % GX)
    up = (ch, ((row + GY - 1) % GY) * GX + col)
    down = (ch, ((row + 1) % GY) * GX + col)
    mate = (h * 2 + (1 - c), tile)
    across = ((1 - h) * 2 + c, tile)

    loads = [
        pltpu.make_async_copy(cached, xin.at[pl.ds(0, 2)], in_sem.at[0]),
        pltpu.make_async_copy(frames, xin.at[pl.ds(2, 2)], in_sem.at[1]),
    ]
    for i, group in enumerate([(1 - h) * 2 + 1 - c, (1 - h) * 2 + c, h * 2 + 1 - c, ch]):
        loads.append(pltpu.make_async_copy(
            weight.at[:, pl.ds(pl.multiple_of(group * CB, CB), CB)], w.at[i // 2, :, pl.ds(i % 2 * CB, CB)], in_sem.at[2 + i]))
    loads.append(pltpu.make_async_copy(bias_in, bias, in_sem.at[6]))
    for load in loads:
        load.start()

    barrier = pltpu.get_barrier_semaphore()
    first_told = h == c

    def tell(semaphore, device):
        pl.semaphore_signal(semaphore, inc=1, device_id=device, device_id_type=MESH)

    @pl.when(jnp.logical_not(first_told))
    def _():
        tell(barrier, mate)
        tell(barrier, across)

    def remote(src, dst, ss, rs, device):
        return pltpu.make_async_remote_copy(src_ref=src, dst_ref=dst, send_sem=ss, recv_sem=rs, device_id=device, device_id_type=MESH)

    def block(i):
        return i, i * BLOCK_ROWS, BLOCK_ROWS

    def half(i):
        return BLOCKS + i, RIM_AT + i * HALF_ROWS, HALF_ROWS

    def end(i):
        return BLOCKS + 2 + i, END_AT + i * END_ROWS, END_ROWS

    def rows_of(at, n):
        return pl.ds(at if isinstance(at, int) else pl.multiple_of(at, 16), n)

    def core(side, part):
        i, at, n = part
        rows = rows_of(at, n)
        return remote(core_out.at[side, rows], core_in.at[side, rows], core_ss.at[side, i], core_rs.at[side, i], mate)

    def cross(part):
        i, at, n = part
        rows = rows_of(at, n)
        return remote(cross_out.at[rows], cross_in.at[rows], cross_ss.at[i], cross_rs.at[i], across)

    def pass_on(part):
        core(0, part).wait_recv()
        rows = rows_of(*part[1:])
        cross_out[rows, :] = encode(keep[0, rows, :] + core_in[0, rows, :])
        cross(part).start()

    def place_of(f, r):
        return f * FRAME + 8 + (r + 1) * TW

    def build(ref, f, q, r):
        for k in range(SLOTS):
            v = xf[pl.ds(place_of(f, r) + k, SLOT, stride=SLOTS), :]
            ref[f, q, (k + 1) * SLOT:(k + 2) * SLOT, :] = v.astype(jnp.bfloat16)

    spot = lax.broadcasted_iota(jnp.int32, (SLOT, CB), 0)

    def build_sides(ref, f, q, r):
        for side, k, slot in ((left_f, -1, 0), (right_f, SLOTS, SLOTS + 1)):
            v = xf[pl.ds(place_of(f, r) + k, SLOT, stride=SLOTS), :]
            at = 0 if k < 0 else 7
            for j in range(2):
                v = jnp.where(spot == at + 8 * j, side[pl.ds(f * SIDE + 8 + r + j, 1), :], v)
            ref[f, q, slot * SLOT:(slot + 1) * SLOT, :] = v.astype(jnp.bfloat16)

    def build_all(q0, q1):
        @pl.loop(q0, q1)
        def _(q):
            for f in range(4):
                build(xo, f, q, 2 * q)
                build(xe, f, q, 2 * q - 1)

    def product(groups, slots, side, at):
        columns = []
        for a, y, e in TAPS:
            pieces = []
            for q, n in groups:
                for first, count in slots:
                    ref, q_at = (xo, q) if y == 1 else (xe, q + y // 2)
                    v = ref[a:a + 2, pl.ds(q_at, n), (first + e) * SLOT:(first + e + count) * SLOT, :]
                    pieces.append(v.reshape(2 * n * count * SLOT, CB))
            columns.append(jnp.concatenate(pieces, axis=0) if len(pieces) > 1 else pieces[0])
        sums = jnp.dot(jnp.concatenate(columns, axis=1), w[side], preferred_element_type=jnp.float32)
        rows = rows_of(at, sums.shape[0])
        core_out[side, rows, :] = sums[:, :CB]
        keep[side, rows, :] = sums[:, CB:]

    loads[0].wait()
    loads[1].wait()

    @pl.loop(0, NP)
    def _(q):
        for f in range(4):
            v = xin[f, pl.ds(pl.multiple_of(q * PAIR, 16), PAIR), :]
            xf[pl.ds(pl.multiple_of(place_of(f, 2 * q), 8), PAIR), :] = v.astype(jnp.float32)

    for f in range(4):
        at = f * TH
        edge_l[at:at + TH, :] = xf[pl.ds(place_of(f, 0), TH, stride=TW), :].astype(jnp.bfloat16)
        edge_r[at:at + TH, :] = xf[pl.ds(place_of(f, 0) + TW - 1, TH, stride=TW), :].astype(jnp.bfloat16)

    @pl.when(first_told)
    def _():
        pl.semaphore_wait(barrier, 2)
        tell(ready.at[0], mate)
        tell(ready.at[1], across)

    build_all(1, 4)

    loads[2].wait()
    loads[3].wait()
    to_left = remote(edge_l, halo_r, halo_ss.at[0], halo_rs.at[0], left)
    to_right = remote(edge_r, halo_l, halo_ss.at[1], halo_rs.at[1], right)
    to_up = remote(xin.at[:, pl.ds(0, 64)], halo_b, halo_ss.at[2], halo_rs.at[2], up)
    to_down = remote(xin.at[:, pl.ds(PIX - 64, 64)], halo_a, halo_ss.at[3], halo_rs.at[3], down)
    halos = (to_left, to_right, to_up, to_down)

    @pl.loop(0, 2 * BLOCKS)
    def _(j):
        side, b = j // BLOCKS, j % BLOCKS

        @pl.when(j == BLOCKS)
        def _():
            loads[4].wait()
            loads[5].wait()

        product([(1 + b * BLOCK, BLOCK)], INNER, side, b * BLOCK_ROWS)

        @pl.when((j == 0) & jnp.logical_not(first_told))
        def _():
            pl.semaphore_wait(ready.at[0], 1)
            for device in (left, right, up, down):
                tell(barrier, device)
            pl.semaphore_wait(ready.at[1], 1)

        core(side, block(b)).start()

        @pl.when((j == HALO_AT) & jnp.logical_not(first_told))
        def _():
            pl.semaphore_wait(barrier, 4)
            tell(ready.at[2], mate)

        @pl.when((j == HALO_AT) & first_told)
        def _():
            pl.semaphore_wait(ready.at[2], 1)

        @pl.when(j == HALO_AT)
        def _():
            for halo in halos:
                halo.start()

        @pl.when(j < BLOCKS - 1)
        def _():
            build_all(2 + (b + 1) * BLOCK, 2 + (b + 2) * BLOCK)

        @pl.when((j > 0) & (j <= BLOCKS))
        def _():
            pass_on(block(j - 1))

    to_left.wait_recv()
    to_right.wait_recv()
    for f in range(4):
        at, to = f * TH, f * SIDE + 8
        left_f[to:to + TH, :] = jnp.where(col > 0, halo_l[at:at + TH, :].astype(jnp.float32), 0.0)
        right_f[to:to + TH, :] = jnp.where(col < GX - 1, halo_r[at:at + TH, :].astype(jnp.float32), 0.0)

    for ref, r in ((corner_up, 0), (corner_dn, TH - 1)):
        pieces = []
        for f in range(4):
            at = f * SIDE + 8 + r
            pieces += [left_f[at:at + 1, :], right_f[at:at + 1, :]]
        ref[...] = jnp.concatenate(pieces + [jnp.zeros((8, CB), jnp.float32)], axis=0).astype(jnp.bfloat16)
    corner_to_up = remote(corner_up, corner_b, halo_ss.at[4], halo_rs.at[4], up)
    corner_to_down = remote(corner_dn, corner_a, halo_ss.at[5], halo_rs.at[5], down)
    corners = (corner_to_up, corner_to_down)
    for corner in corners:
        corner.start()

    @pl.loop(1, NP)
    def _(q):
        for f in range(4):
            build_sides(xo, f, q, 2 * q)
            build_sides(xe, f, q, 2 * q - 1)

    def rim(side):
        @pl.loop(0, 2)
        def _(i):
            product([(1 + i * HALF, HALF)], RIM, side, RIM_AT + i * HALF_ROWS)
            core(side, half(i)).start()

    def both_ends(side):
        product([(0, 1), (NP - 1, 1)], WHOLE, side, END_AT)
        core(side, end(0)).start()
        core(side, end(1)).start()

    rim(0)
    to_up.wait_recv()
    to_down.wait_recv()
    for corner in corners:
        corner.wait_recv()
    above = jnp.where(row > 0, corner_a[...].astype(jnp.float32), 0.0)
    below = jnp.where(row < GY - 1, corner_b[...].astype(jnp.float32), 0.0)
    for f in range(4):
        xf[pl.ds(place_of(f, -1), TW), :] = jnp.where(row > 0, halo_a[f].astype(jnp.float32)[8:], 0.0)
        xf[pl.ds(place_of(f, TH), TW), :] = jnp.where(row < GY - 1, halo_b[f].astype(jnp.float32)[:TW], 0.0)
        at = f * SIDE + 8
        left_f[at - 1:at, :] = above[2 * f:2 * f + 1]
        right_f[at - 1:at, :] = above[2 * f + 1:2 * f + 2]
        left_f[at + TH:at + TH + 1, :] = below[2 * f:2 * f + 1]
        right_f[at + TH:at + TH + 1, :] = below[2 * f + 1:2 * f + 2]
    for f in range(4):
        for ref, q, r in ((xo, 0, 0), (xe, 0, -1), (xe, NP, TH - 1)):
            build(ref, f, q, r)
            build_sides(ref, f, q, r)

    both_ends(0)
    pass_on(half(0))
    pass_on(half(1))
    rim(1)
    pass_on(end(0))
    pass_on(end(1))
    both_ends(1)
    loads[6].wait()

    def finished(at, n):
        rows = pl.ds(at, n)
        v = keep[1, rows, :] + core_in[1, rows, :] + decode(cross_in[rows, :]) + bias[...]
        return v / (1.0 + jnp.exp(-v))

    def spread(v, f, q, k):
        out_f[pl.ds(f * PIX + q * PAIR + k, SLOT, stride=SLOTS), :] = v

    def settle(f, q):
        at = pl.multiple_of(q * PAIR, 16)
        out[f, pl.ds(at, PAIR), :] = out_f[pl.ds(pl.multiple_of(f * PIX + at, 16), PAIR), :].astype(jnp.bfloat16)

    @pl.loop(0, BLOCKS)
    def _(b):
        core(1, block(b)).wait_recv()
        cross(block(b)).wait_recv()
        v = finished(pl.multiple_of(b * BLOCK_ROWS, 16), BLOCK_ROWS)
        for f in range(2):
            for p in range(BLOCK):
                for k in range(5):
                    at = ((f * BLOCK + p) * 5 + k) * SLOT
                    spread(v[at:at + SLOT], f, 1 + b * BLOCK + p, 1 + k)

    @pl.loop(0, 2)
    def _(i):
        core(1, half(i)).wait_recv()
        cross(half(i)).wait_recv()
        v = finished(pl.multiple_of(RIM_AT + i * HALF_ROWS, 16), HALF_ROWS)
        for s, k in enumerate((0, 6)):
            for f in range(2):
                for p in range(HALF):
                    at = ((s * 2 + f) * HALF + p) * SLOT
                    spread(v[at:at + SLOT], f, 1 + i * HALF + p, k)

    @pl.loop(1, NP - 1)
    def _(q):
        for f in range(2):
            settle(f, q)

    for copy in halos + corners:
        copy.wait_send()

    @pl.loop(0, 2)
    def _(i):
        core(1, end(i)).wait_recv()
        cross(end(i)).wait_recv()
        v = finished(pl.multiple_of(END_AT + i * END_ROWS, 16), END_ROWS)
        q = i * (NP - 1)
        for f in range(2):
            for k in range(SLOTS):
                at = (f * SLOTS + k) * SLOT
                spread(v[at:at + SLOT], f, q, k)
            settle(f, q)

    def sent(part):
        core(0, part).wait_send()
        core(1, part).wait_send()
        cross(part).wait_send()

    @pl.loop(0, BLOCKS)
    def _(b):
        sent(block(b))

    for i in range(2):
        sent(half(i))
        sent(end(i))


def shards(frames, cached, weight, out_bias):
    bf16, f32 = jnp.bfloat16, jnp.float32
    operands = (
        cached.reshape(2, PIX, CB),
        frames.reshape(2, PIX, CB),
        weight.reshape(27 * CB, 4 * CB),
        out_bias.reshape(1, CB),
    )
    out = pl.pallas_call(
        kernel,
        out_shape=jax.ShapeDtypeStruct((2, PIX, CB), bf16),
        in_specs=[pl.BlockSpec(memory_space=pl.ANY)] * 4,
        out_specs=pl.BlockSpec(memory_space=pltpu.VMEM),
        scratch_shapes=[
            pltpu.VMEM((4, PIX, CB), bf16),
            pltpu.VMEM((4 * FRAME, CB), f32),
            pltpu.VMEM((4, NP + 1, WIDE, CB), bf16),
            pltpu.VMEM((4, NP, WIDE, CB), bf16),
            pltpu.VMEM((2, 27 * CB, 2 * CB), bf16),
            pltpu.VMEM((1, CB), f32),
            *[pltpu.VMEM((4 * TH, CB), bf16)] * 4,
            *[pltpu.VMEM((4 * SIDE, CB), f32)] * 2,
            *[pltpu.VMEM((4, 64, CB), bf16)] * 2,
            *[pltpu.VMEM((16, CB), bf16)] * 4,
            *[pltpu.VMEM((2, ROWS, CB), f32)] * 3,
            *[pltpu.VMEM((ROWS, CB), bf16)] * 2,
            pltpu.VMEM((2 * PIX, CB), f32),
            pltpu.SemaphoreType.DMA((7,)),
            *[pltpu.SemaphoreType.DMA((6,))] * 2,
            *[pltpu.SemaphoreType.DMA((2, PARTS))] * 2,
            *[pltpu.SemaphoreType.DMA((PARTS,))] * 2,
            pltpu.SemaphoreType.REGULAR((3,)),
        ],
        compiler_params=pltpu.CompilerParams(collective_id=0, has_side_effects=True, vmem_limit_bytes=48 << 20),
        cost_estimate=pl.CostEstimate(flops=2 * 2 * PIX * 27 * CB * 4 * CB, bytes_accessed=7 << 20, transcendentals=2 * PIX * CB),
        name="conv",
    )(*[pltpu.with_memory_space_constraint(x, pltpu.HBM) for x in operands])
    return out.reshape(2, 1, TH, TW, CB)


def solution(mesh):
    in_specs = (
        P(None, "tile", None, None, "ch"),
        P(None, "tile", None, None, "ch"),
        P(None, None, None, "ch", None),
        P("ch"),
    )
    out_specs = P(None, "tile", None, None, "ch")
    return jax.shard_map(shards, mesh=mesh, in_specs=in_specs, out_specs=out_specs, check_vma=False)
```

```python
import jax
import jax.numpy as jnp
from jax import lax
from jax.experimental import pallas as pl
from jax.experimental.pallas import tpu as pltpu
from jax.sharding import PartitionSpec as P

GX = 8
GY = 8
TH = 32
TW = 56
CB = 128
PIX = TH * TW
PAIR = 2 * TW
NP = TH // 2
SLOTS = TW // 8
SLOT = 16
WIDE = (SLOTS + 2) * SLOT
FRAME = 8 + (TH + 2) * TW + 8
SIDE = TH + 16
SCALE = 2.0**20
MESH = pl.DeviceIdType.MESH
TAPS = [(a, b, e) for a in range(3) for b in range(3) for e in range(3)]
INNER = [(1, 5)]
RIM = [(0, 1), (6, 1)]
WHOLE = [(0, 7)]
INNER_ROWS, RIM_ROWS, END_ROWS = 2 * 5 * SLOT, 2 * 2 * SLOT, 2 * PAIR
MIDDLE = NP - 2
RIM_AT = MIDDLE * INNER_ROWS
END_AT = RIM_AT + MIDDLE * RIM_ROWS
ROWS = END_AT + 2 * END_ROWS
BLOCKS = 7
SIDE_AT = 1
HALO_AT = 5
CORNER_AT = 6
BLOCK = MIDDLE // BLOCKS
BLOCK_ROWS = BLOCK * INNER_ROWS
HALF = MIDDLE // 2
HALF_ROWS = HALF * RIM_ROWS
PARTS = BLOCKS + 4


def encode(v):
    s = v * SCALE
    return ((s * s) * (s * jnp.abs(s))).astype(jnp.bfloat16)


def decode(w):
    w = w.astype(jnp.float32)
    root = jnp.sqrt(jnp.sqrt(jnp.abs(w))) * (1.0 / SCALE)
    return jnp.where(w < 0, -root, root)


def kernel(cached, frames, weight, bias_in, out, xin, xf, xe, xo, w, bias, edge_l, edge_r, halo_l, halo_r, left_f, right_f,
           halo_a, halo_b, corner_up, corner_dn, corner_a, corner_b, core_out, core_in, keep, cross_out, cross_in, out_f,
           in_sem, halo_ss, halo_rs, core_ss, core_rs, cross_ss, cross_rs, ready):
    ch = lax.axis_index("ch")
    tile = lax.axis_index("tile")
    h, c = ch // 2, ch % 2
    row, col = tile // GX, tile % GX
    left = (ch, row * GX + (col + GX - 1) % GX)
    right = (ch, row * GX + (col + 1) % GX)
    up = (ch, ((row + GY - 1) % GY) * GX + col)
    down = (ch, ((row + 1) % GY) * GX + col)
    mate = (h * 2 + (1 - c), tile)
    across = ((1 - h) * 2 + c, tile)

    loads = [
        pltpu.make_async_copy(cached, xin.at[pl.ds(0, 2)], in_sem.at[0]),
        pltpu.make_async_copy(frames, xin.at[pl.ds(2, 2)], in_sem.at[1]),
    ]
    for i, group in enumerate([(1 - h) * 2 + 1 - c, (1 - h) * 2 + c, h * 2 + 1 - c, ch]):
        loads.append(pltpu.make_async_copy(
            weight.at[:, pl.ds(pl.multiple_of(group * CB, CB), CB)], w.at[i // 2, :, pl.ds(i % 2 * CB, CB)], in_sem.at[2 + i]))
    loads.append(pltpu.make_async_copy(bias_in, bias, in_sem.at[6]))
    for load in loads:
        load.start()

    barrier = pltpu.get_barrier_semaphore()
    first_told = h == c

    def tell(semaphore, device):
        pl.semaphore_signal(semaphore, inc=1, device_id=device, device_id_type=MESH)

    @pl.when(jnp.logical_not(first_told))
    def _():
        tell(barrier, mate)
        tell(barrier, across)

    def remote(src, dst, ss, rs, device):
        return pltpu.make_async_remote_copy(src_ref=src, dst_ref=dst, send_sem=ss, recv_sem=rs, device_id=device, device_id_type=MESH)

    def block(i):
        return i, i * BLOCK_ROWS, BLOCK_ROWS

    def half(i):
        return BLOCKS + i, RIM_AT + i * HALF_ROWS, HALF_ROWS

    def end(i):
        return BLOCKS + 2 + i, END_AT + i * END_ROWS, END_ROWS

    def rows_of(at, n):
        return pl.ds(at if isinstance(at, int) else pl.multiple_of(at, 16), n)

    def core(side, part):
        i, at, n = part
        rows = rows_of(at, n)
        return remote(core_out.at[side, rows], core_in.at[side, rows], core_ss.at[side, i], core_rs.at[side, i], mate)

    def cross(part):
        i, at, n = part
        rows = rows_of(at, n)
        return remote(cross_out.at[rows], cross_in.at[rows], cross_ss.at[i], cross_rs.at[i], across)

    def pass_on(part):
        core(0, part).wait_recv()
        rows = rows_of(*part[1:])
        cross_out[rows, :] = encode(keep[0, rows, :] + core_in[0, rows, :])
        cross(part).start()

    def place_of(f, r):
        return f * FRAME + 8 + (r + 1) * TW

    def build(ref, f, q, r):
        for k in range(SLOTS):
            v = xf[pl.ds(place_of(f, r) + k, SLOT, stride=SLOTS), :]
            ref[f, q, (k + 1) * SLOT:(k + 2) * SLOT, :] = v.astype(jnp.bfloat16)

    spot = lax.broadcasted_iota(jnp.int32, (SLOT, CB), 0)

    def build_sides(ref, f, q, r):
        for side, k, slot in ((left_f, -1, 0), (right_f, SLOTS, SLOTS + 1)):
            v = xf[pl.ds(place_of(f, r) + k, SLOT, stride=SLOTS), :]
            at = 0 if k < 0 else 7
            for j in range(2):
                v = jnp.where(spot == at + 8 * j, side[pl.ds(f * SIDE + 8 + r + j, 1), :], v)
            ref[f, q, slot * SLOT:(slot + 1) * SLOT, :] = v.astype(jnp.bfloat16)

    def build_all(q0, q1):
        @pl.loop(q0, q1)
        def _(q):
            for f in range(4):
                build(xo, f, q, 2 * q)
                build(xe, f, q, 2 * q - 1)

    def product(groups, slots, side, at):
        columns = []
        for a, y, e in TAPS:
            pieces = []
            for q, n in groups:
                for first, count in slots:
                    ref, q_at = (xo, q) if y == 1 else (xe, q + y // 2)
                    v = ref[a:a + 2, pl.ds(q_at, n), (first + e) * SLOT:(first + e + count) * SLOT, :]
                    pieces.append(v.reshape(2 * n * count * SLOT, CB))
            columns.append(jnp.concatenate(pieces, axis=0) if len(pieces) > 1 else pieces[0])
        sums = jnp.dot(jnp.concatenate(columns, axis=1), w[side], preferred_element_type=jnp.float32)
        rows = rows_of(at, sums.shape[0])
        core_out[side, rows, :] = sums[:, :CB]
        keep[side, rows, :] = sums[:, CB:]

    loads[0].wait()
    loads[1].wait()

    @pl.loop(0, NP)
    def _(q):
        for f in range(4):
            v = xin[f, pl.ds(pl.multiple_of(q * PAIR, 16), PAIR), :]
            xf[pl.ds(pl.multiple_of(place_of(f, 2 * q), 8), PAIR), :] = v.astype(jnp.float32)

    for f in range(4):
        at = f * TH
        edge_l[at:at + TH, :] = xf[pl.ds(place_of(f, 0), TH, stride=TW), :].astype(jnp.bfloat16)
        edge_r[at:at + TH, :] = xf[pl.ds(place_of(f, 0) + TW - 1, TH, stride=TW), :].astype(jnp.bfloat16)

    @pl.when(first_told)
    def _():
        pl.semaphore_wait(barrier, 2)
        tell(ready.at[0], mate)
        tell(ready.at[1], across)

    build_all(1, 4)

    loads[2].wait()
    loads[3].wait()
    to_left = remote(edge_l, halo_r, halo_ss.at[0], halo_rs.at[0], left)
    to_right = remote(edge_r, halo_l, halo_ss.at[1], halo_rs.at[1], right)
    to_up = remote(xin.at[:, pl.ds(0, 64)], halo_b, halo_ss.at[2], halo_rs.at[2], up)
    to_down = remote(xin.at[:, pl.ds(PIX - 64, 64)], halo_a, halo_ss.at[3], halo_rs.at[3], down)
    halos = (to_left, to_right, to_up, to_down)

    corner_to_up = remote(corner_up, corner_b, halo_ss.at[4], halo_rs.at[4], up)
    corner_to_down = remote(corner_dn, corner_a, halo_ss.at[5], halo_rs.at[5], down)
    corners = (corner_to_up, corner_to_down)

    @pl.loop(0, 2 * BLOCKS)
    def _(j):
        side, b = j // BLOCKS, j % BLOCKS

        @pl.when(j == BLOCKS)
        def _():
            loads[4].wait()
            loads[5].wait()

        product([(1 + b * BLOCK, BLOCK)], INNER, side, b * BLOCK_ROWS)

        @pl.when((j == 0) & jnp.logical_not(first_told))
        def _():
            pl.semaphore_wait(ready.at[0], 1)
            pl.semaphore_wait(ready.at[1], 1)

            @pl.when(ch == 1)
            def _():
                tell(barrier, left)
                tell(barrier, right)

            @pl.when(ch == 2)
            def _():
                tell(barrier, up)
                tell(barrier, down)

        core(side, block(b)).start()

        for step, asks, at, pair in ((SIDE_AT, 1, 2, halos[:2]), (HALO_AT, 2, 3, halos[2:])):
            @pl.when((j == step) & (ch == asks))
            def _():
                pl.semaphore_wait(barrier, 2)
                for device in (mate, across, (3 - asks, tile)):
                    tell(ready.at[at], device)

            @pl.when((j == step) & (ch != asks))
            def _():
                pl.semaphore_wait(ready.at[at], 1)

            @pl.when(j == step)
            def _():
                for halo in pair:
                    halo.start()

        @pl.when(j < BLOCKS - 1)
        def _():
            build_all(2 + (b + 1) * BLOCK, 2 + (b + 2) * BLOCK)

        @pl.when((j > 0) & (j <= BLOCKS))
        def _():
            pass_on(block(j - 1))

        @pl.when(j == CORNER_AT)
        def _():
            to_left.wait_recv()
            to_right.wait_recv()
            for f in range(4):
                at, to = f * TH, f * SIDE + 8
                left_f[to:to + TH, :] = jnp.where(col > 0, halo_l[at:at + TH, :].astype(jnp.float32), 0.0)
                right_f[to:to + TH, :] = jnp.where(col < GX - 1, halo_r[at:at + TH, :].astype(jnp.float32), 0.0)

            for ref, r in ((corner_up, 0), (corner_dn, TH - 1)):
                pieces = []
                for f in range(4):
                    at = f * SIDE + 8 + r
                    pieces += [left_f[at:at + 1, :], right_f[at:at + 1, :]]
                ref[...] = jnp.concatenate(pieces + [jnp.zeros((8, CB), jnp.float32)], axis=0).astype(jnp.bfloat16)
            for corner in corners:
                corner.start()

    @pl.loop(1, NP)
    def _(q):
        for f in range(4):
            build_sides(xo, f, q, 2 * q)
            build_sides(xe, f, q, 2 * q - 1)

    def rim(side):
        @pl.loop(0, 2)
        def _(i):
            product([(1 + i * HALF, HALF)], RIM, side, RIM_AT + i * HALF_ROWS)
            core(side, half(i)).start()

    def both_ends(side):
        product([(0, 1), (NP - 1, 1)], WHOLE, side, END_AT)
        core(side, end(0)).start()
        core(side, end(1)).start()

    rim(0)
    to_up.wait_recv()
    to_down.wait_recv()
    for corner in corners:
        corner.wait_recv()
    above = jnp.where(row > 0, corner_a[...].astype(jnp.float32), 0.0)
    below = jnp.where(row < GY - 1, corner_b[...].astype(jnp.float32), 0.0)
    for f in range(4):
        xf[pl.ds(place_of(f, -1), TW), :] = jnp.where(row > 0, halo_a[f].astype(jnp.float32)[8:], 0.0)
        xf[pl.ds(place_of(f, TH), TW), :] = jnp.where(row < GY - 1, halo_b[f].astype(jnp.float32)[:TW], 0.0)
        at = f * SIDE + 8
        left_f[at - 1:at, :] = above[2 * f:2 * f + 1]
        right_f[at - 1:at, :] = above[2 * f + 1:2 * f + 2]
        left_f[at + TH:at + TH + 1, :] = below[2 * f:2 * f + 1]
        right_f[at + TH:at + TH + 1, :] = below[2 * f + 1:2 * f + 2]
    for f in range(4):
        for ref, q, r in ((xo, 0, 0), (xe, 0, -1), (xe, NP, TH - 1)):
            build(ref, f, q, r)
            build_sides(ref, f, q, r)

    both_ends(0)
    pass_on(half(0))
    pass_on(half(1))
    rim(1)
    pass_on(end(0))
    pass_on(end(1))
    both_ends(1)
    loads[6].wait()

    def finished(at, n):
        rows = pl.ds(at, n)
        v = keep[1, rows, :] + core_in[1, rows, :] + decode(cross_in[rows, :]) + bias[...]
        return v / (1.0 + jnp.exp(-v))

    def spread(v, f, q, k):
        out_f[pl.ds(f * PIX + q * PAIR + k, SLOT, stride=SLOTS), :] = v

    def settle(f, q):
        at = pl.multiple_of(q * PAIR, 16)
        out[f, pl.ds(at, PAIR), :] = out_f[pl.ds(pl.multiple_of(f * PIX + at, 16), PAIR), :].astype(jnp.bfloat16)

    @pl.loop(0, BLOCKS)
    def _(b):
        core(1, block(b)).wait_recv()
        cross(block(b)).wait_recv()
        v = finished(pl.multiple_of(b * BLOCK_ROWS, 16), BLOCK_ROWS)
        for f in range(2):
            for p in range(BLOCK):
                for k in range(5):
                    at = ((f * BLOCK + p) * 5 + k) * SLOT
                    spread(v[at:at + SLOT], f, 1 + b * BLOCK + p, 1 + k)

    @pl.loop(0, 2)
    def _(i):
        core(1, half(i)).wait_recv()
        cross(half(i)).wait_recv()
        v = finished(pl.multiple_of(RIM_AT + i * HALF_ROWS, 16), HALF_ROWS)
        for s, k in enumerate((0, 6)):
            for f in range(2):
                for p in range(HALF):
                    at = ((s * 2 + f) * HALF + p) * SLOT
                    spread(v[at:at + SLOT], f, 1 + i * HALF + p, k)

    @pl.loop(1, NP - 1)
    def _(q):
        for f in range(2):
            settle(f, q)

    for copy in halos + corners:
        copy.wait_send()

    @pl.loop(0, 2)
    def _(i):
        core(1, end(i)).wait_recv()
        cross(end(i)).wait_recv()
        v = finished(pl.multiple_of(END_AT + i * END_ROWS, 16), END_ROWS)
        q = i * (NP - 1)
        for f in range(2):
            for k in range(SLOTS):
                at = (f * SLOTS + k) * SLOT
                spread(v[at:at + SLOT], f, q, k)
            settle(f, q)

    def sent(part):
        core(0, part).wait_send()
        core(1, part).wait_send()
        cross(part).wait_send()

    @pl.loop(0, BLOCKS)
    def _(b):
        sent(block(b))

    for i in range(2):
        sent(half(i))
        sent(end(i))


def shards(frames, cached, weight, out_bias):
    bf16, f32 = jnp.bfloat16, jnp.float32
    operands = (
        cached.reshape(2, PIX, CB),
        frames.reshape(2, PIX, CB),
        weight.reshape(27 * CB, 4 * CB),
        out_bias.reshape(1, CB),
    )
    out = pl.pallas_call(
        kernel,
        out_shape=jax.ShapeDtypeStruct((2, PIX, CB), bf16),
        in_specs=[pl.BlockSpec(memory_space=pl.ANY)] * 4,
        out_specs=pl.BlockSpec(memory_space=pltpu.VMEM),
        scratch_shapes=[
            pltpu.VMEM((4, PIX, CB), bf16),
            pltpu.VMEM((4 * FRAME, CB), f32),
            pltpu.VMEM((4, NP + 1, WIDE, CB), bf16),
            pltpu.VMEM((4, NP, WIDE, CB), bf16),
            pltpu.VMEM((2, 27 * CB, 2 * CB), bf16),
            pltpu.VMEM((1, CB), f32),
            *[pltpu.VMEM((4 * TH, CB), bf16)] * 4,
            *[pltpu.VMEM((4 * SIDE, CB), f32)] * 2,
            *[pltpu.VMEM((4, 64, CB), bf16)] * 2,
            *[pltpu.VMEM((16, CB), bf16)] * 4,
            *[pltpu.VMEM((2, ROWS, CB), f32)] * 3,
            *[pltpu.VMEM((ROWS, CB), bf16)] * 2,
            pltpu.VMEM((2 * PIX, CB), f32),
            pltpu.SemaphoreType.DMA((7,)),
            *[pltpu.SemaphoreType.DMA((6,))] * 2,
            *[pltpu.SemaphoreType.DMA((2, PARTS))] * 2,
            *[pltpu.SemaphoreType.DMA((PARTS,))] * 2,
            pltpu.SemaphoreType.REGULAR((4,)),
        ],
        compiler_params=pltpu.CompilerParams(collective_id=0, has_side_effects=True, vmem_limit_bytes=48 << 20),
        cost_estimate=pl.CostEstimate(flops=2 * 2 * PIX * 27 * CB * 4 * CB, bytes_accessed=7 << 20, transcendentals=2 * PIX * CB),
        name="conv",
    )(*[pltpu.with_memory_space_constraint(x, pltpu.HBM) for x in operands])
    return out.reshape(2, 1, TH, TW, CB)


def solution(mesh):
    in_specs = (
        P(None, "tile", None, None, "ch"),
        P(None, "tile", None, None, "ch"),
        P(None, None, None, "ch", None),
        P("ch"),
    )
    out_specs = P(None, "tile", None, None, "ch")
    return jax.shard_map(shards, mesh=mesh, in_specs=in_specs, out_specs=out_specs, check_vma=False)
```

```python
import jax
import jax.numpy as jnp
from jax import lax
from jax.experimental import pallas as pl
from jax.experimental.pallas import tpu as pltpu
from jax.sharding import PartitionSpec as P

GX = 8
GY = 8
TH = 32
TW = 56
CB = 128
PIX = TH * TW
PAIR = 2 * TW
NP = TH // 2
SLOTS = TW // 8
SLOT = 16
WIDE = (SLOTS + 2) * SLOT
FRAME = 8 + (TH + 2) * TW + 8
SIDE = TH + 16
SCALE = 2.0**20
MESH = pl.DeviceIdType.MESH
TAPS = [(a, b, e) for a in range(3) for b in range(3) for e in range(3)]
INNER = [(1, 5)]
RIM = [(0, 1), (6, 1)]
WHOLE = [(0, 7)]
INNER_ROWS, RIM_ROWS, END_ROWS = 2 * 5 * SLOT, 2 * 2 * SLOT, 2 * PAIR
MIDDLE = NP - 2
RIM_AT = MIDDLE * INNER_ROWS
END_AT = RIM_AT + MIDDLE * RIM_ROWS
ROWS = END_AT + 2 * END_ROWS
BLOCKS = 7
CORNER_AT = 5
BLOCK = MIDDLE // BLOCKS
BLOCK_ROWS = BLOCK * INNER_ROWS
HALF = MIDDLE // 2
HALF_ROWS = HALF * RIM_ROWS
PARTS = BLOCKS + 4


def encode(v):
    s = v * SCALE
    return ((s * s) * (s * jnp.abs(s))).astype(jnp.bfloat16)


def decode(w):
    w = w.astype(jnp.float32)
    root = jnp.sqrt(jnp.sqrt(jnp.abs(w))) * (1.0 / SCALE)
    return jnp.where(w < 0, -root, root)


def kernel(cached, frames, weight, bias_in, out, xin, xf, xe, xo, w, bias, edge_l, edge_r, halo_l, halo_r, left_f, right_f,
           halo_a, halo_b, corner_up, corner_dn, corner_a, corner_b, core_out, core_in, keep, cross_out, cross_in, out_f,
           in_sem, halo_ss, halo_rs, core_ss, core_rs, cross_ss, cross_rs):
    ch = lax.axis_index("ch")
    tile = lax.axis_index("tile")
    h, c = ch // 2, ch % 2
    row, col = tile // GX, tile % GX
    left = (ch, row * GX + (col + GX - 1) % GX)
    right = (ch, row * GX + (col + 1) % GX)
    up = (ch, ((row + GY - 1) % GY) * GX + col)
    down = (ch, ((row + 1) % GY) * GX + col)
    mate = (h * 2 + (1 - c), tile)
    across = ((1 - h) * 2 + c, tile)

    loads = [
        pltpu.make_async_copy(cached, xin.at[pl.ds(0, 2)], in_sem.at[0]),
        pltpu.make_async_copy(frames, xin.at[pl.ds(2, 2)], in_sem.at[1]),
    ]
    for i, group in enumerate([(1 - h) * 2 + 1 - c, (1 - h) * 2 + c, h * 2 + 1 - c, ch]):
        loads.append(pltpu.make_async_copy(
            weight.at[:, pl.ds(pl.multiple_of(group * CB, CB), CB)], w.at[i // 2, :, pl.ds(i % 2 * CB, CB)], in_sem.at[2 + i]))
    loads.append(pltpu.make_async_copy(bias_in, bias, in_sem.at[6]))
    for load in loads:
        load.start()

    barrier = pltpu.get_barrier_semaphore()
    for device in (left, right, up, down, mate, across):
        pl.semaphore_signal(barrier, inc=1, device_id=device, device_id_type=MESH)

    def remote(src, dst, ss, rs, device):
        return pltpu.make_async_remote_copy(src_ref=src, dst_ref=dst, send_sem=ss, recv_sem=rs, device_id=device, device_id_type=MESH)

    def block(i):
        return i, i * BLOCK_ROWS, BLOCK_ROWS

    def half(i):
        return BLOCKS + i, RIM_AT + i * HALF_ROWS, HALF_ROWS

    def end(i):
        return BLOCKS + 2 + i, END_AT + i * END_ROWS, END_ROWS

    def rows_of(at, n):
        return pl.ds(at if isinstance(at, int) else pl.multiple_of(at, 16), n)

    def core(side, part):
        i, at, n = part
        rows = rows_of(at, n)
        return remote(core_out.at[side, rows], core_in.at[side, rows], core_ss.at[side, i], core_rs.at[side, i], mate)

    def cross(part):
        i, at, n = part
        rows = rows_of(at, n)
        return remote(cross_out.at[rows], cross_in.at[rows], cross_ss.at[i], cross_rs.at[i], across)

    def pass_on(part):
        core(0, part).wait_recv()
        rows = rows_of(*part[1:])
        cross_out[rows, :] = encode(keep[0, rows, :] + core_in[0, rows, :])
        cross(part).start()

    def place_of(f, r):
        return f * FRAME + 8 + (r + 1) * TW

    def build(ref, f, q, r):
        for k in range(SLOTS):
            v = xf[pl.ds(place_of(f, r) + k, SLOT, stride=SLOTS), :]
            ref[f, q, (k + 1) * SLOT:(k + 2) * SLOT, :] = v.astype(jnp.bfloat16)

    spot = lax.broadcasted_iota(jnp.int32, (SLOT, CB), 0)

    def build_sides(ref, f, q, r):
        for side, k, slot in ((left_f, -1, 0), (right_f, SLOTS, SLOTS + 1)):
            v = xf[pl.ds(place_of(f, r) + k, SLOT, stride=SLOTS), :]
            at = 0 if k < 0 else 7
            for j in range(2):
                v = jnp.where(spot == at + 8 * j, side[pl.ds(f * SIDE + 8 + r + j, 1), :], v)
            ref[f, q, slot * SLOT:(slot + 1) * SLOT, :] = v.astype(jnp.bfloat16)

    def build_all(q0, q1):
        @pl.loop(q0, q1)
        def _(q):
            for f in range(4):
                build(xo, f, q, 2 * q)
                build(xe, f, q, 2 * q - 1)

    def product(groups, slots, side, at):
        columns = []
        for a, y, e in TAPS:
            pieces = []
            for q, n in groups:
                for first, count in slots:
                    ref, q_at = (xo, q) if y == 1 else (xe, q + y // 2)
                    v = ref[a:a + 2, pl.ds(q_at, n), (first + e) * SLOT:(first + e + count) * SLOT, :]
                    pieces.append(v.reshape(2 * n * count * SLOT, CB))
            columns.append(jnp.concatenate(pieces, axis=0) if len(pieces) > 1 else pieces[0])
        sums = jnp.dot(jnp.concatenate(columns, axis=1), w[side], preferred_element_type=jnp.float32)
        rows = rows_of(at, sums.shape[0])
        core_out[side, rows, :] = sums[:, :CB]
        keep[side, rows, :] = sums[:, CB:]

    loads[0].wait()
    loads[1].wait()

    @pl.loop(0, NP)
    def _(q):
        for f in range(4):
            v = xin[f, pl.ds(pl.multiple_of(q * PAIR, 16), PAIR), :]
            xf[pl.ds(pl.multiple_of(place_of(f, 2 * q), 8), PAIR), :] = v.astype(jnp.float32)

    for f in range(4):
        at = f * TH
        edge_l[at:at + TH, :] = xf[pl.ds(place_of(f, 0), TH, stride=TW), :].astype(jnp.bfloat16)
        edge_r[at:at + TH, :] = xf[pl.ds(place_of(f, 0) + TW - 1, TH, stride=TW), :].astype(jnp.bfloat16)

    build_all(1, 4)
    loads[2].wait()
    loads[3].wait()
    to_left = remote(edge_l, halo_r, halo_ss.at[0], halo_rs.at[0], left)
    to_right = remote(edge_r, halo_l, halo_ss.at[1], halo_rs.at[1], right)
    to_up = remote(xin.at[:, pl.ds(0, 64)], halo_b, halo_ss.at[2], halo_rs.at[2], up)
    to_down = remote(xin.at[:, pl.ds(PIX - 64, 64)], halo_a, halo_ss.at[3], halo_rs.at[3], down)
    halos = (to_left, to_right, to_up, to_down)

    corner_to_up = remote(corner_up, corner_b, halo_ss.at[4], halo_rs.at[4], up)
    corner_to_down = remote(corner_dn, corner_a, halo_ss.at[5], halo_rs.at[5], down)
    corners = (corner_to_up, corner_to_down)

    @pl.loop(0, 2 * BLOCKS)
    def _(j):
        side, b = j // BLOCKS, j % BLOCKS

        @pl.when(j == BLOCKS)
        def _():
            loads[4].wait()
            loads[5].wait()

        product([(1 + b * BLOCK, BLOCK)], INNER, side, b * BLOCK_ROWS)

        @pl.when(j == 0)
        def _():
            pl.semaphore_wait(barrier, 6)
            core(side, block(b)).start()
            for halo in halos:
                halo.start()

        @pl.when(j > 0)
        def _():
            core(side, block(b)).start()

        @pl.when(j < BLOCKS - 1)
        def _():
            build_all(2 + (b + 1) * BLOCK, 2 + (b + 2) * BLOCK)

        @pl.when((j > 0) & (j <= BLOCKS))
        def _():
            pass_on(block(j - 1))

        @pl.when(j == CORNER_AT)
        def _():
            to_left.wait_recv()
            to_right.wait_recv()
            for f in range(4):
                at, to = f * TH, f * SIDE + 8
                left_f[to:to + TH, :] = jnp.where(col > 0, halo_l[at:at + TH, :].astype(jnp.float32), 0.0)
                right_f[to:to + TH, :] = jnp.where(col < GX - 1, halo_r[at:at + TH, :].astype(jnp.float32), 0.0)

            for ref, r in ((corner_up, 0), (corner_dn, TH - 1)):
                pieces = []
                for f in range(4):
                    at = f * SIDE + 8 + r
                    pieces += [left_f[at:at + 1, :], right_f[at:at + 1, :]]
                ref[...] = jnp.concatenate(pieces + [jnp.zeros((8, CB), jnp.float32)], axis=0).astype(jnp.bfloat16)
            for corner in corners:
                corner.start()

    @pl.loop(1, NP)
    def _(q):
        for f in range(4):
            build_sides(xo, f, q, 2 * q)
            build_sides(xe, f, q, 2 * q - 1)

    def rim(side):
        @pl.loop(0, 2)
        def _(i):
            product([(1 + i * HALF, HALF)], RIM, side, RIM_AT + i * HALF_ROWS)
            core(side, half(i)).start()

    def both_ends(side):
        product([(0, 1), (NP - 1, 1)], WHOLE, side, END_AT)
        core(side, end(0)).start()
        core(side, end(1)).start()

    rim(0)
    to_up.wait_recv()
    to_down.wait_recv()
    for corner in corners:
        corner.wait_recv()
    above = jnp.where(row > 0, corner_a[...].astype(jnp.float32), 0.0)
    below = jnp.where(row < GY - 1, corner_b[...].astype(jnp.float32), 0.0)
    for f in range(4):
        xf[pl.ds(place_of(f, -1), TW), :] = jnp.where(row > 0, halo_a[f].astype(jnp.float32)[8:], 0.0)
        xf[pl.ds(place_of(f, TH), TW), :] = jnp.where(row < GY - 1, halo_b[f].astype(jnp.float32)[:TW], 0.0)
        at = f * SIDE + 8
        left_f[at - 1:at, :] = above[2 * f:2 * f + 1]
        right_f[at - 1:at, :] = above[2 * f + 1:2 * f + 2]
        left_f[at + TH:at + TH + 1, :] = below[2 * f:2 * f + 1]
        right_f[at + TH:at + TH + 1, :] = below[2 * f + 1:2 * f + 2]
    for f in range(4):
        for ref, q, r in ((xo, 0, 0), (xe, 0, -1), (xe, NP, TH - 1)):
            build(ref, f, q, r)
            build_sides(ref, f, q, r)

    both_ends(0)
    pass_on(half(0))
    pass_on(half(1))
    rim(1)
    pass_on(end(0))
    pass_on(end(1))
    both_ends(1)
    loads[6].wait()

    def finished(at, n):
        rows = pl.ds(at, n)
        v = keep[1, rows, :] + core_in[1, rows, :] + decode(cross_in[rows, :]) + bias[...]
        return v / (1.0 + jnp.exp(-v))

    def spread(v, f, q, k):
        out_f[pl.ds(f * PIX + q * PAIR + k, SLOT, stride=SLOTS), :] = v

    def settle(f, q):
        at = pl.multiple_of(q * PAIR, 16)
        out[f, pl.ds(at, PAIR), :] = out_f[pl.ds(pl.multiple_of(f * PIX + at, 16), PAIR), :].astype(jnp.bfloat16)

    @pl.loop(0, BLOCKS)
    def _(b):
        core(1, block(b)).wait_recv()
        cross(block(b)).wait_recv()
        v = finished(pl.multiple_of(b * BLOCK_ROWS, 16), BLOCK_ROWS)
        for f in range(2):
            for p in range(BLOCK):
                for k in range(5):
                    at = ((f * BLOCK + p) * 5 + k) * SLOT
                    spread(v[at:at + SLOT], f, 1 + b * BLOCK + p, 1 + k)

    @pl.loop(0, 2)
    def _(i):
        core(1, half(i)).wait_recv()
        cross(half(i)).wait_recv()
        v = finished(pl.multiple_of(RIM_AT + i * HALF_ROWS, 16), HALF_ROWS)
        for s, k in enumerate((0, 6)):
            for f in range(2):
                for p in range(HALF):
                    at = ((s * 2 + f) * HALF + p) * SLOT
                    spread(v[at:at + SLOT], f, 1 + i * HALF + p, k)

    @pl.loop(1, NP - 1)
    def _(q):
        for f in range(2):
            settle(f, q)

    for copy in halos + corners:
        copy.wait_send()

    @pl.loop(0, 2)
    def _(i):
        core(1, end(i)).wait_recv()
        cross(end(i)).wait_recv()
        v = finished(pl.multiple_of(END_AT + i * END_ROWS, 16), END_ROWS)
        q = i * (NP - 1)
        for f in range(2):
            for k in range(SLOTS):
                at = (f * SLOTS + k) * SLOT
                spread(v[at:at + SLOT], f, q, k)
            settle(f, q)

    def sent(part):
        core(0, part).wait_send()
        core(1, part).wait_send()
        cross(part).wait_send()

    @pl.loop(0, BLOCKS)
    def _(b):
        sent(block(b))

    for i in range(2):
        sent(half(i))
        sent(end(i))


def shards(frames, cached, weight, out_bias):
    bf16, f32 = jnp.bfloat16, jnp.float32
    operands = (
        cached.reshape(2, PIX, CB),
        frames.reshape(2, PIX, CB),
        weight.reshape(27 * CB, 4 * CB),
        out_bias.reshape(1, CB),
    )
    out = pl.pallas_call(
        kernel,
        out_shape=jax.ShapeDtypeStruct((2, PIX, CB), bf16),
        in_specs=[pl.BlockSpec(memory_space=pl.ANY)] * 4,
        out_specs=pl.BlockSpec(memory_space=pltpu.VMEM),
        scratch_shapes=[
            pltpu.VMEM((4, PIX, CB), bf16),
            pltpu.VMEM((4 * FRAME, CB), f32),
            pltpu.VMEM((4, NP + 1, WIDE, CB), bf16),
            pltpu.VMEM((4, NP, WIDE, CB), bf16),
            pltpu.VMEM((2, 27 * CB, 2 * CB), bf16),
            pltpu.VMEM((1, CB), f32),
            *[pltpu.VMEM((4 * TH, CB), bf16)] * 4,
            *[pltpu.VMEM((4 * SIDE, CB), f32)] * 2,
            *[pltpu.VMEM((4, 64, CB), bf16)] * 2,
            *[pltpu.VMEM((16, CB), bf16)] * 4,
            *[pltpu.VMEM((2, ROWS, CB), f32)] * 3,
            *[pltpu.VMEM((ROWS, CB), bf16)] * 2,
            pltpu.VMEM((2 * PIX, CB), f32),
            pltpu.SemaphoreType.DMA((7,)),
            *[pltpu.SemaphoreType.DMA((6,))] * 2,
            *[pltpu.SemaphoreType.DMA((2, PARTS))] * 2,
            *[pltpu.SemaphoreType.DMA((PARTS,))] * 2,
        ],
        compiler_params=pltpu.CompilerParams(collective_id=0, has_side_effects=True, vmem_limit_bytes=48 << 20),
        cost_estimate=pl.CostEstimate(flops=2 * 2 * PIX * 27 * CB * 4 * CB, bytes_accessed=7 << 20, transcendentals=2 * PIX * CB),
        name="conv",
    )(*[pltpu.with_memory_space_constraint(x, pltpu.HBM) for x in operands])
    return out.reshape(2, 1, TH, TW, CB)


def solution(mesh):
    in_specs = (
        P(None, "tile", None, None, "ch"),
        P(None, "tile", None, None, "ch"),
        P(None, None, None, "ch", None),
        P("ch"),
    )
    out_specs = P(None, "tile", None, None, "ch")
    return jax.shard_map(shards, mesh=mesh, in_specs=in_specs, out_specs=out_specs, check_vma=False)
```
